32 devices in a mesh: grp: 4 (over x, core), dev: 8 (over z, y).
Axes of the slice: x: 2, y: 2, z: 4, core: 2. Of those that a mesh axis runs over, the one named last changes fastest.
Arguments:
- fine_residual: bfloat16 [4, 8, 4, 4, 24, 2, 3072], P('grp', 'dev'), may hold values from -4 to 4
- near_null: bfloat16 [4, 8, 4, 4, 2, 32, 3072], P('grp', 'dev'), may hold values from -0.375 to 0.375
- coarse_operator: bfloat16 [4, 8, 4, 4, 64, 1152], P(None, 'dev'), may hold values from -1 to 7
Outputs:
- fine_correction: bfloat16 [4, 8, 4, 4, 24, 2, 3072], P('grp', 'dev')
- coarse_residual: float32 [4, 8, 4, 4, 24, 128], P('grp', 'dev')
The draws below stay inside these ranges and needn't reach their ends.
All inputs are finite; a program needn't handle non-finite values.
Results may differ from the reference program's by a relative error of at most 0.012.
The reference program's roundings to bfloat16 on the way count: a program that leaves them out, or rounds other values in their place, can miss the bound.
Values may be sent and summed in bfloat16 or wider, within the bound.
No kernel may reach another device: no remote copies, remote signals or barrier semaphores. Data moves between devices by JAX's collectives and lax.ppermute only.
A program may use at most 128 MiB of HBM per device.

```python
import functools
import math
import jax
import jax.numpy as jnp
from jax import lax

NVEC = 32
COARSE = 64
SPINCOL = 12
BLOCK = 256
NRHS = 24
LY = 4
LX = 4
ITERS = 3
LT = 4
LZ = 8


def draw_fine_residual(key, part):
    extent = (LT, LZ, LY, LX, NRHS, 2, SPINCOL * BLOCK)
    depth = jnp.arange(LZ, dtype=jnp.float32).reshape(1, LZ, 1, 1, 1, 1, 1) / max(LZ - 1, 1)
    former = jax.random.fold_in(key, 0)
    gradient = jnp.exp(depth * math.log(10.0))
    values = 0.12 * gradient * jax.random.normal(former, extent, jnp.float32)
    return jnp.clip(values, -4.0, 4.0).astype(jnp.bfloat16)


def draw_coarse_operator(key, part):
    rows = COARSE
    cols = 18 * COARSE
    extent = (LT, LZ, LY, LX, rows, cols)
    spread = 0.4 / math.sqrt(18.0 * COARSE)
    former, latter = jax.random.split(key)
    row_ids = lax.broadcasted_iota(jnp.int32, (rows, cols), 0)
    col_ids = lax.broadcasted_iota(jnp.int32, (rows, cols), 1)
    on_diag = (row_ids == col_ids).astype(jnp.float32)
    depth = jnp.arange(LZ, dtype=jnp.float32).reshape(1, LZ, 1, 1, 1, 1) / max(LZ - 1, 1)
    rising = 1.0 + 2.0 * depth
    jitter = jnp.clip(jax.random.normal(former, extent, jnp.float32), -4.0, 4.0) * spread
    diagonal_level = jax.random.uniform(latter, (LT, LZ, LY, LX, rows, 1), jnp.float32, 1.0, 2.0)
    return (jitter + rising * diagonal_level * on_diag).astype(jnp.bfloat16)


def steps_of(rng, shape, cuts, smallest, high):
    loudness = 1.0
    for position, blocks in cuts:
        steps = jax.random.uniform(jax.random.fold_in(jax.random.fold_in(rng, 6), position), (blocks,), jnp.float32, smallest / len(cuts), high / len(cuts))
        loudness = loudness * jnp.repeat(jnp.exp(steps), shape[position] // blocks).reshape((-1,) + (1,) * (len(shape) - 1 - position))
    return loudness


def centred(own_key, dims, width, limit, pieces=(), held_as=jnp.bfloat16):
    array = jax.random.normal(own_key, dims, jnp.float32) * width
    if len(pieces) > 0:
        array = steps_of(own_key, dims, pieces, -0.22, 0.18) * array
    return jnp.clip(array, min=-limit, max=limit).astype(held_as)


def setup_inputs(seed: int = 0) -> dict:
    arg_keys = jax.random.split(jax.random.key(seed), 4)
    return {
        "fine_residual": draw_fine_residual(jax.random.fold_in(arg_keys[3], 71), 0),
        "near_null": centred(arg_keys[1], (LT, LZ, LY, LX, 2, NVEC, SPINCOL * BLOCK), BLOCK ** -0.5, 0.375, ((0, 4), (1, 8))),
        "coarse_operator": draw_coarse_operator(jax.random.fold_in(arg_keys[3], 71), 0),
    }


def complex_columns(piece, ncoarse):
    real_part = piece[..., :ncoarse]
    imag_part = piece[..., ncoarse:]
    former = jnp.concatenate([real_part, -imag_part], axis=-1)
    latter = jnp.concatenate([imag_part, real_part], axis=-1)
    return jnp.stack([former, latter], axis=-2)


def restrict_plane(operands):
    vectors, field = operands
    middle = vectors.shape[-1] // 2
    vectors = vectors.astype(jnp.float32)
    field = field.astype(jnp.float32)
    upper = jnp.einsum("zyxpkm,zyxnqm->zyxnpqk", vectors[..., :middle], field[..., :middle])
    lower = jnp.einsum("zyxpkm,zyxnqm->zyxnpqk", vectors[..., middle:], field[..., middle:])
    joined = jnp.concatenate([upper, lower], axis=-1)
    real_part = joined[..., 0, 0, :] + joined[..., 1, 1, :]
    imag_part = joined[..., 0, 1, :] - joined[..., 1, 0, :]
    return jnp.concatenate([real_part, imag_part], axis=-1)


def coefficients(solution, first_index, last_index, ncoarse):
    real_part = solution[..., first_index:last_index]
    imag_part = solution[..., ncoarse + first_index:ncoarse + last_index]
    former = jnp.stack([real_part, -imag_part], axis=-2)
    latter = jnp.stack([imag_part, real_part], axis=-2)
    return jnp.stack([former, latter], axis=-3)


def prolong_plane(operands):
    vectors, rounded = operands
    vector_count = vectors.shape[-2]
    ncoarse = 2 * vector_count
    middle = vectors.shape[-1] // 2
    vectors = vectors.astype(jnp.float32)
    upper = jnp.einsum("zyxnqpk,zyxpkm->zyxnqm", coefficients(rounded, 0, vector_count, ncoarse).astype(jnp.float32), vectors[..., :middle])
    lower = jnp.einsum("zyxnqpk,zyxpkm->zyxnqm", coefficients(rounded, vector_count, ncoarse, ncoarse).astype(jnp.float32), vectors[..., middle:])
    return jnp.concatenate([upper, lower], axis=-1).astype(jnp.bfloat16)


def apply_plane(operands):
    blocks, columns = operands
    leading = blocks.shape[:3]
    sites_total = leading[0] * leading[1] * leading[2]
    ncoarse = blocks.shape[-2]
    blocks = blocks.reshape(sites_total, ncoarse, 9, 2 * ncoarse).astype(jnp.float32)
    columns = columns.reshape((sites_total,) + columns.shape[3:]).astype(jnp.float32)
    result = jnp.einsum("sidk,sdnqk->snqi", blocks, columns)
    return result.reshape(leading + (result.shape[1], 2 * ncoarse))


def coarse_apply(operator, vector, ncoarse):
    rounded = vector.astype(jnp.bfloat16)
    shifted = [rounded]
    for dimension in range(4):
        shifted.append(jnp.roll(rounded, -1, dimension))
        shifted.append(jnp.roll(rounded, 1, dimension))
    columns = complex_columns(jnp.stack(shifted, axis=4), ncoarse)
    return lax.map(apply_plane, (operator, columns))


def inner_terms(left, right, ncoarse):
    left_re = left[..., :ncoarse]
    left_im = left[..., ncoarse:]
    right_re = right[..., :ncoarse]
    right_im = right[..., ncoarse:]
    summed = (0, 1, 2, 3, 5)
    return jnp.stack([jnp.sum(left_re * right_re + left_im * right_im, axis=summed),
                      jnp.sum(left_re * right_im - left_im * right_re, axis=summed)])


def scaled(coef, vector, ncoarse):
    coef_real = coef[0][:, None]
    coef_imag = coef[1][:, None]
    vec_real = vector[..., :ncoarse]
    vec_imag = vector[..., ncoarse:]
    return jnp.concatenate([coef_real * vec_real - coef_imag * vec_imag,
                            coef_real * vec_imag + coef_imag * vec_real], axis=-1)


def reference(fine_residual, near_null, coarse_operator):
    ncoarse = 2 * near_null.shape[-2]
    source = lax.map(restrict_plane, (near_null, fine_residual))
    apply_fn = functools.partial(coarse_apply, coarse_operator, ncoarse=ncoarse)
    solution = jnp.zeros_like(source)
    residual = source
    directions = []
    images = []
    curvatures = []
    for iteration in range(ITERS):
        direction = residual
        product = apply_fn(direction)
        correlations = [inner_terms(earlier_q, product, ncoarse) for earlier_q in images]
        for earlier in range(iteration):
            factor = correlations[earlier] / curvatures[earlier][None, :]
            product = product - scaled(factor, images[earlier], ncoarse)
            direction = direction - scaled(factor, directions[earlier], ncoarse)
        curvature = inner_terms(product, product, ncoarse)[0]
        along = inner_terms(product, residual, ncoarse)
        step_size = along / curvature[None, :]
        solution = solution + scaled(step_size, direction, ncoarse)
        residual = residual - scaled(step_size, product, ncoarse)
        directions.append(direction)
        images.append(product)
        curvatures.append(curvature)
    rounded = solution.astype(jnp.bfloat16)
    fine_correction = lax.map(prolong_plane, (near_null, rounded))
    return fine_correction, residual
```

```python
import functools

import jax
import jax.numpy as jnp
from jax import lax
from jax.experimental import pallas as pl
from jax.experimental.pallas import tpu as pltpu
from jax.sharding import PartitionSpec as P

ITERS = 3
SHIFT = 3.0
LIMIT = 40 * 1024 * 1024
F32 = jnp.float32
BF16 = jnp.bfloat16
NT = (((1,), (1,)), ((), ()))
NN = (((1,), (0,)), ((), ()))
VM = pl.BlockSpec(memory_space=pltpu.VMEM)
ANY = pl.BlockSpec(memory_space=pl.ANY)
PARAMS = pltpu.CompilerParams(vmem_limit_bytes=LIMIT)


def pairings(count):
    if count % 2:
        ahead = [(i, (i - 1) % count) for i in range(count)]
        return ahead, [(target, source) for source, target in ahead]
    first = [(i, i ^ 1) for i in range(count)]
    second = [(i, (i + 1) % count if i % 2 else (i - 1) % count) for i in range(count)]
    return first, second


def swapped(axis):
    if lax.axis_size(axis) % 2:
        return jnp.bool_(False)
    return lax.rem(lax.axis_index(axis), 2) == 1


def exchange(high):
    planes = {}
    for axis in ("dev", "grp"):
        first, second = pairings(lax.axis_size(axis))
        planes[axis] = (lax.ppermute(high, axis, second), lax.ppermute(high, axis, first))
    return planes["grp"][1], planes["grp"][0], planes["dev"][1], planes["dev"][0]


def lanes(shape):
    return lax.broadcasted_iota(jnp.int32, shape, len(shape) - 1)


def stacked(vector):
    wide = vector.astype(F32)
    half = wide.shape[-1] // 2
    turned = pltpu.roll(wide, half, 1)
    sign = jnp.where(lanes(wide.shape) < half, 1.0, -1.0)
    return jnp.concatenate([wide * sign, turned], axis=0).astype(BF16)


def halves(value):
    high = value.astype(BF16)
    return high, (value - high.astype(F32)).astype(BF16)


def joined(product, rows):
    return jnp.concatenate([product[:rows], product[rows:]], axis=1)


def restrict_kernel(field_hbm, near_hbm, source_ref, high_ref, low_ref, near_ref, field, prods, sem):
    sites = field.shape[0]
    nrhs = field.shape[1]
    middle = field.shape[-1] // 2
    copies = []
    for s in range(sites):
        pair = (
            pltpu.make_async_copy(field_hbm.at[s], field.at[s], sem.at[0, s]),
            pltpu.make_async_copy(near_hbm.at[s], near_ref.at[s], sem.at[1, s]),
        )
        for copy in pair:
            copy.start()
        copies.append(pair)
    nvec = near_ref.shape[1] // 2
    for s in range(sites):
        for copy in copies[s]:
            copy.wait()
        fine = field[s].reshape(2 * nrhs, 2 * middle)
        near = near_ref[s]
        parts = [
            lax.dot_general(
                fine[:, h * middle : (h + 1) * middle],
                near[:, h * middle : (h + 1) * middle],
                NT,
                preferred_element_type=F32,
            )
            for h in range(2)
        ]
        prods[s] = jnp.concatenate(parts, axis=1)
    for s in range(sites):
        even = prods[s, pl.ds(0, nrhs, 2), :]
        odd = prods[s, pl.ds(1, nrhs, 2), :]
        wide = 4 * nvec
        real = even + pltpu.roll(odd, wide - nvec, 1)
        imag = odd - pltpu.roll(even, wide - nvec, 1)
        lane = lanes(real.shape)
        value = jnp.where(
            lane < nvec,
            real,
            jnp.where(
                lane < 2 * nvec,
                pltpu.roll(real, wide - nvec, 1),
                jnp.where(lane < 3 * nvec, pltpu.roll(imag, 2 * nvec, 1), pltpu.roll(imag, nvec, 1)),
            ),
        )
        source_ref[s] = value
        high, low = halves(value)
        high_ref[s] = high
        low_ref[s] = low


def restrict(field, near):
    sites, nrhs, _, fine = field.shape
    coarse = 2 * near.shape[1]
    return pl.pallas_call(
        restrict_kernel,
        in_specs=[ANY, ANY],
        out_specs=[VM] * 4,
        out_shape=[
            jax.ShapeDtypeStruct((sites, nrhs, coarse), F32),
            jax.ShapeDtypeStruct((sites, nrhs, coarse), BF16),
            jax.ShapeDtypeStruct((sites, nrhs, coarse), BF16),
            jax.ShapeDtypeStruct(near.shape, BF16),
        ],
        scratch_shapes=[
            pltpu.VMEM(field.shape, BF16),
            pltpu.VMEM((sites, 2 * nrhs, coarse), F32),
            pltpu.SemaphoreType.DMA((2, sites)),
        ],
        compiler_params=PARAMS,
        name="restrict",
    )(field, near)


def neighbours(s, ly, lx):
    y, x = s // lx, s % lx
    return [((y + 1) % ly) * lx + x, ((y - 1) % ly) * lx + x, y * lx + (x + 1) % lx, y * lx + (x - 1) % lx]


def local_product(s, dims, blocks, xy, extra):
    rows = xy.shape[1]
    wide = xy.shape[2]
    centre = lax.dot_general(
        jnp.concatenate([xy[s]] + [stacked(e) for e in extra], axis=0),
        blocks[:, :wide],
        NT,
        preferred_element_type=F32,
    )
    sides = lax.dot_general(
        jnp.concatenate([xy[j] for j in neighbours(s, *dims)], axis=1),
        blocks[:, 5 * wide :],
        NT,
        preferred_element_type=F32,
    )
    total = centre[:rows] + sides
    return total, [centre[(i + 1) * rows : (i + 2) * rows] for i in range(len(extra))]


def first_local_kernel(dims, high, low, oper_hbm, part_ref, rest_ref, oper_ref, xy, sem):
    sites = xy.shape[0]
    copies = []
    plane = lax.axis_index("grp")
    for s in range(sites):
        copy = pltpu.make_async_copy(oper_hbm.at[plane, s], oper_ref.at[s], sem.at[s])
        copy.start()
        copies.append(copy)
    for s in range(sites):
        xy[s] = stacked(high[s])
    rows = high.shape[1]
    for s in range(sites):
        copies[s].wait()
        total, extra = local_product(s, dims, oper_ref[s], xy, [low[s]])
        part_ref[s] = joined(total, rows)
        rest_ref[s] = joined(extra[0], rows)


def later_local_kernel(dims, with_rest, high, low, *refs):
    if with_rest:
        rest, oper_ref, part_ref, rest_out, xy = refs
    else:
        oper_ref, part_ref, xy = refs
    sites = xy.shape[0]
    rows = high.shape[1]
    for s in range(sites):
        xy[s] = stacked(high[s])
    for s in range(sites):
        extra = [low[s]] + ([rest[s]] if with_rest else [])
        total, more = local_product(s, dims, oper_ref[s], xy, extra)
        part_ref[s] = joined(total + more[0], rows)
        if with_rest:
            rest_out[s] = joined(more[1], rows)


def halo_value(s, flips, planes, part, before, oper_ref):
    rows, wide = part.shape[1], part.shape[2]
    cols = []
    for flip, (one, two) in zip(flips, planes):
        a, b = one[s].astype(F32), two[s].astype(F32)
        cols.append(stacked(jnp.where(flip, b, a)))
        cols.append(stacked(jnp.where(flip, a, b)))
    product = lax.dot_general(
        jnp.concatenate(cols, axis=1), oper_ref[s, :, wide : 5 * wide], NT, preferred_element_type=F32
    )
    return part[s] + joined(product, rows) - SHIFT * before[s]


def halo_kernel(t_one, t_two, z_one, z_two, part, before, oper_ref, value_ref, high_ref, low_ref):
    flips = (swapped("grp"), swapped("dev"))
    for s in range(part.shape[0]):
        value = halo_value(s, flips, ((t_one, t_two), (z_one, z_two)), part, before, oper_ref)
        value_ref[s] = value
        high_ref[s], low_ref[s] = halves(value)


def slots(count):
    table = {}
    for i in range(count):
        for j in range(i, count):
            table[(i, j, 0)] = len(table)
            if j > i:
                table[(i, j, 1)] = len(table)
    return table


def last_kernel(t_one, t_two, z_one, z_two, part, r0, v1, w1, v2, w2, oper_ref, v3, sums_ref):
    flips = (swapped("grp"), swapped("dev"))
    sites, rows, wide = part.shape
    half = wide // 2
    for s in range(sites):
        v3[s] = halo_value(s, flips, ((t_one, t_two), (z_one, z_two)), part, v2, oper_ref)
    basis = [r0, v1, w1, v2, w2, v3]
    table = slots(len(basis))
    total = {key: jnp.zeros((rows, wide), F32) for key in table}
    for s in range(sites):
        plain = [b[s] for b in basis]
        turned = [pltpu.roll(p, half, 1) for p in plain]
        for i, j, part_of in table:
            total[(i, j, part_of)] += plain[i] * (turned[j] if part_of else plain[j])
    sign = jnp.where(lanes((rows, wide)) < half, 1.0, -1.0)
    lane = lanes((rows, wide))
    packed = jnp.zeros((rows, wide), F32)
    for key, slot in table.items():
        value = total[key] * sign if key[2] else total[key]
        packed = jnp.where(lane == slot, jnp.sum(value, axis=1, keepdims=True), packed)
    square = jnp.concatenate([packed, jnp.zeros((wide - rows, wide), F32)], axis=0).T
    dense = jnp.zeros((8, wide), F32)
    for group in range(-(-len(table) // 8)):
        piece = square[8 * group : 8 * group + 8]
        dense = dense + (pltpu.roll(piece, rows * group, 1) if group else piece)
    for d in range(sums_ref.shape[0]):
        sums_ref[d] = dense


def times(a, b):
    return (a[0] * b[0] - a[1] * b[1], a[0] * b[1] + a[1] * b[0])


def plus(a, b):
    return (a[0] + b[0], a[1] + b[1])


def minus(a, b):
    return (a[0] - b[0], a[1] - b[1])


def over(a, b):
    return (a[0] / b, a[1] / b)


def combine(a, b, op):
    out = []
    for x, y in zip(a, b):
        if y is None:
            out.append(x)
        elif x is None:
            out.append(y if op is plus else (-y[0], -y[1]))
        else:
            out.append(op(x, y))
    return out


def scale(c, a):
    return [None if x is None else times(c, x) for x in a]


def recurrences(gram, one):
    zero = jnp.zeros_like(one)

    def entry(i, j):
        if i == j:
            return (gram[(i, i, 0)], zero)
        if i < j:
            return (gram[(i, j, 0)], gram[(i, j, 1)])
        return (gram[(j, i, 0)], -gram[(j, i, 1)])

    count = 6

    def lower(a):
        out = []
        for i in range(count):
            total = (zero, zero)
            for j in range(count):
                if a[j] is not None:
                    total = plus(total, times(entry(i, j), a[j]))
            out.append(total)
        return out

    def inner(a, lowered):
        total = (zero, zero)
        for x, y in zip(a, lowered):
            if x is not None:
                total = plus(total, times((x[0], -x[1]), y))
        return total

    def apply(a, rounded):
        out = [None] * count
        shift = lambda x: (SHIFT * x[0], SHIFT * x[1])
        for source, target in ((0, 1), (1, 3), (3, 5)):
            if a[source] is not None:
                out = combine(out, [shift(a[source]) if k == source else None for k in range(count)], plus)
                out = combine(out, [a[source] if k == target else None for k in range(count)], plus)
        if a[0] is not None and not rounded:
            out = combine(out, [a[0] if k == 2 else None for k in range(count)], plus)
        if a[2] is not None:
            out = combine(out, [a[2] if k == 4 else None for k in range(count)], plus)
        return out

    residual = [(one, zero)] + [None] * (count - 1)
    answer = [None] * count
    directions, images, lows, curvatures = [], [], [], []
    for iteration in range(ITERS):
        direction = residual
        image = apply(direction, iteration == 0)
        factors = [over(inner(image, low), c) for low, c in zip(lows, curvatures)]
        factors = [(f[0], -f[1]) for f in factors]
        for f, p, q in zip(factors, directions, images):
            image = combine(image, scale(f, q), minus)
            direction = combine(direction, scale(f, p), minus)
        low = lower(image)
        curvature = inner(image, low)[0]
        along = inner(residual, low)
        step = over((along[0], -along[1]), curvature)
        answer = combine(answer, scale(step, direction), plus)
        residual = combine(residual, scale(step, image), minus)
        directions.append(direction)
        images.append(image)
        lows.append(low)
        curvatures.append(curvature)
    return answer, residual


def finish_kernel(sums, r0, v1, w1, v2, w2, v3, near, fine_hbm, resid_ref, coef, fine, sem):
    sites, rows, wide = r0.shape
    half = wide // 2
    quarter = half // 2
    middle = near.shape[-1] // 2
    dense = sums[0]
    for d in range(1, sums.shape[0]):
        dense = dense + sums[d]
    basis = [r0, v1, w1, v2, w2, v3]
    table = slots(len(basis))
    turned = [dense if g == 0 else pltpu.roll(dense, wide - rows * g, 1) for g in range(-(-len(table) // 8))]
    gram = {key: turned[slot // 8][slot % 8 : slot % 8 + 1] for key, slot in table.items()}
    answer, residual = recurrences(gram, jnp.ones((1, wide), F32))
    entries = []
    for which, coords in ((0, answer), (1, residual)):
        for index, value in enumerate(coords):
            if value is not None:
                entries.append((which, index, value))
    coef[...] = jnp.zeros_like(coef)
    for e, (_, _, value) in enumerate(entries):
        coef[2 * e : 2 * e + 1] = value[0]
        coef[2 * e + 1 : 2 * e + 2] = value[1]
    columns = coef[...].T[:rows]
    sign = jnp.where(lanes((rows, wide)) < half, -1.0, 1.0)
    spread = [
        (
            which,
            index,
            jnp.broadcast_to(columns[:, 2 * e : 2 * e + 1], (rows, wide)),
            jnp.broadcast_to(columns[:, 2 * e + 1 : 2 * e + 2], (rows, wide)) * sign,
        )
        for e, (which, index, _) in enumerate(entries)
    ]
    lane = lanes((rows, wide))
    copies = []
    for s in range(sites):
        plain = [b[s] for b in basis]
        rolled = [pltpu.roll(p, half, 1) for p in plain]
        out = [jnp.zeros((rows, wide), F32), jnp.zeros((rows, wide), F32)]
        for which, index, re, im in spread:
            out[which] = out[which] + re * plain[index] + im * rolled[index]
        resid_ref[s] = out[1]
        x = out[0].astype(BF16).astype(F32)
        by1 = pltpu.roll(x, wide - quarter, 1)
        by2 = pltpu.roll(x, half, 1)
        by3 = pltpu.roll(x, quarter, 1)
        upper = (jnp.where(lane < quarter, x, -by1), jnp.where(lane < quarter, by2, by3))
        lower = (jnp.where(lane < quarter, by1, -by2), jnp.where(lane < quarter, by3, x))
        for h, (first, second) in enumerate((upper, lower)):
            mixed = jnp.stack([first, second], axis=1).reshape(2 * rows, wide)[:, :half].astype(BF16)
            product = lax.dot_general(
                mixed, near[s, :, h * middle : (h + 1) * middle], NN, preferred_element_type=F32
            )
            fine[s, :, :, h * middle : (h + 1) * middle] = product.astype(BF16).reshape(rows, 2, middle)
        copy = pltpu.make_async_copy(fine.at[s], fine_hbm.at[s], sem.at[s])
        copy.start()
        copies.append(copy)
    for copy in copies:
        copy.wait()


def on_device(fine_residual, near_null, coarse_operator):
    ly, lx, nrhs, _, fine = fine_residual.shape[2:]
    sites = ly * lx
    nvec = near_null.shape[-2]
    wide = 4 * nvec
    field = fine_residual.reshape(sites, nrhs, 2, fine)
    near = near_null.reshape(sites, 2 * nvec, fine)
    oper = coarse_operator.reshape((-1, sites) + coarse_operator.shape[-2:])
    dims = (ly, lx)
    vector = jax.ShapeDtypeStruct((sites, nrhs, wide), F32)
    rounded = jax.ShapeDtypeStruct((sites, nrhs, wide), BF16)
    xy = pltpu.VMEM((sites, 2 * nrhs, wide), BF16)

    r0, h0, l0, near = restrict(field, near)

    planes = exchange(h0)
    part, w1, oper = pl.pallas_call(
        functools.partial(first_local_kernel, dims),
        in_specs=[VM, VM, ANY],
        out_specs=[VM] * 3,
        out_shape=[vector, vector, jax.ShapeDtypeStruct(oper.shape[1:], BF16)],
        scratch_shapes=[xy, pltpu.SemaphoreType.DMA((sites,))],
        compiler_params=PARAMS,
        name="local_1",
    )(h0, l0, oper)
    v1, h1, l1 = pl.pallas_call(
        halo_kernel,
        in_specs=[VM] * 7,
        out_specs=[VM] * 3,
        out_shape=[vector, rounded, rounded],
        compiler_params=PARAMS,
        name="halo_1",
    )(*planes, part, r0, oper)

    planes = exchange(h1)
    part, w2 = pl.pallas_call(
        functools.partial(later_local_kernel, dims, True),
        in_specs=[VM] * 4,
        out_specs=[VM] * 2,
        out_shape=[vector, vector],
        scratch_shapes=[xy],
        compiler_params=PARAMS,
        name="local_2",
    )(h1, l1, w1, oper)
    v2, h2, l2 = pl.pallas_call(
        halo_kernel,
        in_specs=[VM] * 7,
        out_specs=[VM] * 3,
        out_shape=[vector, rounded, rounded],
        compiler_params=PARAMS,
        name="halo_2",
    )(*planes, part, v1, oper)

    planes = exchange(h2)
    part = pl.pallas_call(
        functools.partial(later_local_kernel, dims, False),
        in_specs=[VM] * 3,
        out_specs=VM,
        out_shape=vector,
        scratch_shapes=[xy],
        compiler_params=PARAMS,
        name="local_3",
    )(h2, l2, oper)
    devices = lax.axis_size("grp") * lax.axis_size("dev")
    v3, sums = pl.pallas_call(
        last_kernel,
        in_specs=[VM] * 11,
        out_specs=[VM] * 2,
        out_shape=[vector, jax.ShapeDtypeStruct((devices, 8, wide), F32)],
        compiler_params=PARAMS,
        name="halo_3",
    )(*planes, part, r0, v1, w1, v2, w2, oper)

    sums = lax.all_to_all(sums, ("grp", "dev"), 0, 0)
    correction, residual = pl.pallas_call(
        finish_kernel,
        in_specs=[VM] * 8,
        out_specs=[ANY, VM],
        out_shape=[jax.ShapeDtypeStruct(field.shape, BF16), vector],
        scratch_shapes=[
            pltpu.VMEM((wide, wide), F32),
            pltpu.VMEM(field.shape, BF16),
            pltpu.SemaphoreType.DMA((sites,)),
        ],
        compiler_params=PARAMS,
        name="finish",
    )(sums, r0, v1, w1, v2, w2, v3, near)
    return correction.reshape(fine_residual.shape), residual.reshape((1, 1, ly, lx, nrhs, wide))


def solution(mesh):
    in_specs = (
        P("grp", "dev", None, None, None, None, None),
        P("grp", "dev", None, None, None, None, None),
        P(None, "dev", None, None, None, None),
    )
    out_specs = (
        P("grp", "dev", None, None, None, None, None),
        P("grp", "dev", None, None, None, None),
    )
    return jax.shard_map(
        on_device, mesh=mesh, in_specs=in_specs, out_specs=out_specs, check_vma=False
    )
```

```python
import functools

import jax
import jax.numpy as jnp
from jax import lax
from jax.experimental import pallas as pl
from jax.experimental.pallas import tpu as pltpu
from jax.sharding import PartitionSpec as P

ITERS = 3
SHIFT = 3.0
EACH = 2
LIMIT = 16 * 1024 * 1024
F32 = jnp.float32
BF16 = jnp.bfloat16
NT = (((1,), (1,)), ((), ()))
NN = (((1,), (0,)), ((), ()))
VM = pl.BlockSpec(memory_space=pltpu.VMEM)
HBM = pl.BlockSpec(memory_space=pltpu.HBM)
PARAMS = pltpu.CompilerParams(vmem_limit_bytes=LIMIT)


def pairings(count):
    if count % 2:
        ahead = [(i, (i - 1) % count) for i in range(count)]
        return ahead, [(target, source) for source, target in ahead]
    first = [(i, i ^ 1) for i in range(count)]
    second = [(i, (i + 1) % count if i % 2 else (i - 1) % count) for i in range(count)]
    return first, second


def swapped(axis):
    if lax.axis_size(axis) % 2:
        return jnp.bool_(False)
    return lax.rem(lax.axis_index(axis), 2) == 1


def exchange(high):
    planes = {}
    for axis in ("dev", "grp"):
        first, second = pairings(lax.axis_size(axis))
        planes[axis] = (lax.ppermute(high, axis, second), lax.ppermute(high, axis, first))
    return planes["grp"][1], planes["grp"][0], planes["dev"][1], planes["dev"][0]


def lanes(shape):
    return lax.broadcasted_iota(jnp.int32, shape, len(shape) - 1)


def stacked(vector):
    wide = vector.astype(F32)
    half = wide.shape[-1] // 2
    turned = pltpu.roll(wide, half, 1)
    sign = jnp.where(lanes(wide.shape) < half, 1.0, -1.0)
    return jnp.concatenate([wide * sign, turned], axis=0).astype(BF16)


def halves(value):
    high = value.astype(BF16)
    return high, (value - high.astype(F32)).astype(BF16)


def joined(product, rows):
    return jnp.concatenate([product[:rows], product[rows:]], axis=1)


def restrict_kernel(
    field_hbm, near_hbm, oper_hbm, source_ref, high_ref, low_ref, near_ref, oper_ref, field, prods, sem, oper_sem
):
    sites, nrhs = field.shape[:2]
    middle = field.shape[-1] // 2
    nvec = near_ref.shape[1] // 2
    wide = 4 * nvec
    groups = sem.shape[1]
    each = EACH
    copies = []
    for g in range(groups):
        span = pl.ds(g * each, each)
        pair = (
            pltpu.make_async_copy(field_hbm.at[span], field.at[span], sem.at[0, g]),
            pltpu.make_async_copy(near_hbm.at[span], near_ref.at[span], sem.at[1, g]),
        )
        for copy in pair:
            copy.start()
        copies.append(pair)
    last = pltpu.make_async_copy(oper_hbm.at[lax.axis_index("grp")], oper_ref, oper_sem)
    last.start()
    lane = lanes((nrhs, wide))

    def multiply(s):
        fine = field[s].reshape(2 * nrhs, 2 * middle)
        near = near_ref[s]
        parts = [
            lax.dot_general(
                fine[:, h * middle : (h + 1) * middle],
                near[:, h * middle : (h + 1) * middle],
                NT,
                preferred_element_type=F32,
            )
            for h in range(2)
        ]
        prods[s] = jnp.concatenate(parts, axis=1)

    def arrange(s):
        even = prods[s, pl.ds(0, nrhs, 2), :]
        odd = prods[s, pl.ds(1, nrhs, 2), :]
        real = even + pltpu.roll(odd, wide - nvec, 1)
        imag = odd - pltpu.roll(even, wide - nvec, 1)
        value = jnp.where(
            lane < nvec,
            real,
            jnp.where(
                lane < 2 * nvec,
                pltpu.roll(real, wide - nvec, 1),
                jnp.where(lane < 3 * nvec, pltpu.roll(imag, 2 * nvec, 1), pltpu.roll(imag, nvec, 1)),
            ),
        )
        source_ref[s] = value
        high_ref[s], low_ref[s] = halves(value)

    for g in range(groups + 1):
        if g < groups:
            for copy in copies[g]:
                copy.wait()
            for s in range(g * each, (g + 1) * each):
                multiply(s)
        if g:
            for s in range((g - 1) * each, g * each):
                arrange(s)
    last.wait()


def restrict(field, near, oper):
    sites, nrhs, _, fine = field.shape
    coarse = 2 * near.shape[1]
    return pl.pallas_call(
        restrict_kernel,
        in_specs=[HBM] * 3,
        out_specs=[VM] * 5,
        out_shape=[
            jax.ShapeDtypeStruct((sites, nrhs, coarse), F32),
            jax.ShapeDtypeStruct((sites, nrhs, coarse), BF16),
            jax.ShapeDtypeStruct((sites, nrhs, coarse), BF16),
            jax.ShapeDtypeStruct(near.shape, BF16),
            jax.ShapeDtypeStruct(oper.shape[1:], BF16),
        ],
        scratch_shapes=[
            pltpu.VMEM(field.shape, BF16),
            pltpu.VMEM((sites, 2 * nrhs, coarse), F32),
            pltpu.SemaphoreType.DMA((2, sites // EACH)),
            pltpu.SemaphoreType.DMA,
        ],
        compiler_params=PARAMS,
        name="restrict",
    )(field, near, oper)


def neighbours(s, ly, lx):
    y, x = s // lx, s % lx
    return [((y + 1) % ly) * lx + x, ((y - 1) % ly) * lx + x, y * lx + (x + 1) % lx, y * lx + (x - 1) % lx]


def local_product(s, dims, blocks, xy, extra):
    rows = xy.shape[1]
    wide = xy.shape[2]
    centre = lax.dot_general(
        jnp.concatenate([xy[s]] + [stacked(e) for e in extra], axis=0),
        blocks[:, :wide],
        NT,
        preferred_element_type=F32,
    )
    sides = lax.dot_general(
        jnp.concatenate([xy[j] for j in neighbours(s, *dims)], axis=1),
        blocks[:, 5 * wide :],
        NT,
        preferred_element_type=F32,
    )
    total = centre[:rows] + sides
    return total, [centre[(i + 1) * rows : (i + 2) * rows] for i in range(len(extra))]


def first_local_kernel(dims, high, low, oper_ref, part_ref, rest_ref, xy):
    sites = xy.shape[0]
    rows = high.shape[1]
    for s in range(sites):
        xy[s] = stacked(high[s])
    for s in range(sites):
        total, extra = local_product(s, dims, oper_ref[s], xy, [low[s]])
        part_ref[s] = joined(total, rows)
        rest_ref[s] = joined(extra[0], rows)


def later_local_kernel(dims, with_rest, high, low, *refs):
    if with_rest:
        rest, oper_ref, part_ref, rest_out, xy = refs
    else:
        oper_ref, part_ref, xy = refs
    sites = xy.shape[0]
    rows = high.shape[1]
    for s in range(sites):
        xy[s] = stacked(high[s])
    for s in range(sites):
        extra = [low[s]] + ([rest[s]] if with_rest else [])
        total, more = local_product(s, dims, oper_ref[s], xy, extra)
        part_ref[s] = joined(total + more[0], rows)
        if with_rest:
            rest_out[s] = joined(more[1], rows)


def halo_value(s, flips, planes, part, before, oper_ref):
    rows, wide = part.shape[1], part.shape[2]
    cols = []
    for flip, (one, two) in zip(flips, planes):
        a, b = one[s].astype(F32), two[s].astype(F32)
        cols.append(stacked(jnp.where(flip, b, a)))
        cols.append(stacked(jnp.where(flip, a, b)))
    product = lax.dot_general(
        jnp.concatenate(cols, axis=1), oper_ref[s, :, wide : 5 * wide], NT, preferred_element_type=F32
    )
    return part[s] + joined(product, rows) - SHIFT * before[s]


def halo_kernel(t_one, t_two, z_one, z_two, part, before, oper_ref, value_ref, high_ref, low_ref):
    flips = (swapped("grp"), swapped("dev"))
    for s in range(part.shape[0]):
        value = halo_value(s, flips, ((t_one, t_two), (z_one, z_two)), part, before, oper_ref)
        value_ref[s] = value
        high_ref[s], low_ref[s] = halves(value)


def slots(count):
    table = {}
    for i in range(count):
        for j in range(i, count):
            table[(i, j, 0)] = len(table)
            if j > i:
                table[(i, j, 1)] = len(table)
    return table


def last_kernel(t_one, t_two, z_one, z_two, part, r0, v1, w1, v2, w2, oper_ref, v3, sums_ref):
    flips = (swapped("grp"), swapped("dev"))
    sites, rows, wide = part.shape
    half = wide // 2
    for s in range(sites):
        v3[s] = halo_value(s, flips, ((t_one, t_two), (z_one, z_two)), part, v2, oper_ref)
    basis = [r0, v1, w1, v2, w2, v3]
    table = slots(len(basis))
    total = {key: jnp.zeros((rows, wide), F32) for key in table}
    for s in range(sites):
        plain = [b[s] for b in basis]
        turned = [pltpu.roll(p, half, 1) for p in plain]
        for i, j, part_of in table:
            total[(i, j, part_of)] += plain[i] * (turned[j] if part_of else plain[j])
    sign = jnp.where(lanes((rows, wide)) < half, 1.0, -1.0)
    lane = lanes((rows, wide))
    packed = jnp.zeros((rows, wide), F32)
    for key, slot in table.items():
        value = total[key] * sign if key[2] else total[key]
        packed = jnp.where(lane == slot, jnp.sum(value, axis=1, keepdims=True), packed)
    square = jnp.concatenate([packed, jnp.zeros((wide - rows, wide), F32)], axis=0).T
    dense = jnp.zeros((8, wide), F32)
    for group in range(-(-len(table) // 8)):
        piece = square[8 * group : 8 * group + 8]
        dense = dense + (pltpu.roll(piece, rows * group, 1) if group else piece)
    for d in range(sums_ref.shape[0]):
        sums_ref[d] = dense


def times(a, b):
    return (a[0] * b[0] - a[1] * b[1], a[0] * b[1] + a[1] * b[0])


def plus(a, b):
    return (a[0] + b[0], a[1] + b[1])


def minus(a, b):
    return (a[0] - b[0], a[1] - b[1])


def over(a, b):
    return (a[0] / b, a[1] / b)


def combine(a, b, op):
    out = []
    for x, y in zip(a, b):
        if y is None:
            out.append(x)
        elif x is None:
            out.append(y if op is plus else (-y[0], -y[1]))
        else:
            out.append(op(x, y))
    return out


def scale(c, a):
    return [None if x is None else times(c, x) for x in a]


def recurrences(gram, one):
    zero = jnp.zeros_like(one)

    def entry(i, j):
        if i == j:
            return (gram[(i, i, 0)], zero)
        if i < j:
            return (gram[(i, j, 0)], gram[(i, j, 1)])
        return (gram[(j, i, 0)], -gram[(j, i, 1)])

    count = 6

    def lower(a):
        out = []
        for i in range(count):
            total = (zero, zero)
            for j in range(count):
                if a[j] is not None:
                    total = plus(total, times(entry(i, j), a[j]))
            out.append(total)
        return out

    def inner(a, lowered):
        total = (zero, zero)
        for x, y in zip(a, lowered):
            if x is not None:
                total = plus(total, times((x[0], -x[1]), y))
        return total

    def apply(a, rounded):
        out = [None] * count
        shift = lambda x: (SHIFT * x[0], SHIFT * x[1])
        for source, target in ((0, 1), (1, 3), (3, 5)):
            if a[source] is not None:
                out = combine(out, [shift(a[source]) if k == source else None for k in range(count)], plus)
                out = combine(out, [a[source] if k == target else None for k in range(count)], plus)
        if a[0] is not None and not rounded:
            out = combine(out, [a[0] if k == 2 else None for k in range(count)], plus)
        if a[2] is not None:
            out = combine(out, [a[2] if k == 4 else None for k in range(count)], plus)
        return out

    residual = [(one, zero)] + [None] * (count - 1)
    answer = [None] * count
    directions, images, lows, curvatures = [], [], [], []
    for iteration in range(ITERS):
        direction = residual
        image = apply(direction, iteration == 0)
        factors = [over(inner(image, low), c) for low, c in zip(lows, curvatures)]
        factors = [(f[0], -f[1]) for f in factors]
        for f, p, q in zip(factors, directions, images):
            image = combine(image, scale(f, q), minus)
            direction = combine(direction, scale(f, p), minus)
        low = lower(image)
        curvature = inner(image, low)[0]
        along = inner(residual, low)
        step = over((along[0], -along[1]), curvature)
        answer = combine(answer, scale(step, direction), plus)
        residual = combine(residual, scale(step, image), minus)
        directions.append(direction)
        images.append(image)
        lows.append(low)
        curvatures.append(curvature)
    return answer, residual


def finish_kernel(sums, r0, v1, w1, v2, w2, v3, near, fine_hbm, resid_hbm, coef, mixed, fine, resid, sem, resid_sem):
    sites, rows, wide = r0.shape
    half = wide // 2
    quarter = half // 2
    middle = near.shape[-1] // 2
    dense = sums[0]
    for d in range(1, sums.shape[0]):
        dense = dense + sums[d]
    basis = [r0, v1, w1, v2, w2, v3]
    table = slots(len(basis))
    turned = [dense if g == 0 else pltpu.roll(dense, wide - rows * g, 1) for g in range(-(-len(table) // 8))]
    gram = {key: turned[slot // 8][slot % 8 : slot % 8 + 1] for key, slot in table.items()}
    answer, residual = recurrences(gram, jnp.ones((1, wide), F32))
    entries = []
    for which, coords in ((0, answer), (1, residual)):
        for index, value in enumerate(coords):
            if value is not None:
                entries.append((which, index, value))
    coef[...] = jnp.zeros_like(coef)
    for e, (_, _, value) in enumerate(entries):
        coef[2 * e : 2 * e + 1] = value[0]
        coef[2 * e + 1 : 2 * e + 2] = value[1]
    columns = coef[...].T[:rows]
    sign = jnp.where(lanes((rows, wide)) < half, -1.0, 1.0)
    spread = [
        (
            which,
            index,
            jnp.broadcast_to(columns[:, 2 * e : 2 * e + 1], (rows, wide)),
            jnp.broadcast_to(columns[:, 2 * e + 1 : 2 * e + 2], (rows, wide)) * sign,
        )
        for e, (which, index, _) in enumerate(entries)
    ]
    lane = lanes((rows, wide))
    def combined(s):
        plain = [b[s] for b in basis]
        rolled = [pltpu.roll(p, half, 1) for p in plain]
        out = [jnp.zeros((rows, wide), F32), jnp.zeros((rows, wide), F32)]
        for which, index, re, im in spread:
            out[which] = out[which] + re * plain[index] + im * rolled[index]
        resid[s] = out[1]
        x = out[0].astype(BF16).astype(F32)
        by1 = pltpu.roll(x, wide - quarter, 1)
        by2 = pltpu.roll(x, half, 1)
        by3 = pltpu.roll(x, quarter, 1)
        mixed[s, 0, pl.ds(0, rows, 2), :] = jnp.where(lane < quarter, x, -by1)
        mixed[s, 0, pl.ds(1, rows, 2), :] = jnp.where(lane < quarter, by2, by3)
        mixed[s, 1, pl.ds(0, rows, 2), :] = jnp.where(lane < quarter, by1, -by2)
        mixed[s, 1, pl.ds(1, rows, 2), :] = jnp.where(lane < quarter, by3, x)

    def prolonged(s):
        for h in range(2):
            cols = slice(h * middle, (h + 1) * middle)
            product = lax.dot_general(
                mixed[s, h, :, :half].astype(BF16), near[s, :, cols], NN, preferred_element_type=F32
            )
            fine[s, :, :, cols] = product.astype(BF16).reshape(rows, 2, middle)

    groups = sem.shape[0]
    copies = []
    for g in range(groups + 1):
        if g < groups:
            for s in range(g * EACH, (g + 1) * EACH):
                combined(s)
        if g == groups - 1:
            copies.append(pltpu.make_async_copy(resid, resid_hbm, resid_sem))
            copies[-1].start()
        if g:
            span = pl.ds((g - 1) * EACH, EACH)
            for s in range((g - 1) * EACH, g * EACH):
                prolonged(s)
            copies.append(pltpu.make_async_copy(fine.at[span], fine_hbm.at[span], sem.at[g - 1]))
            copies[-1].start()
    for copy in copies:
        copy.wait()


def finish(sums, *arrays):
    sites, nrhs, wide = arrays[0].shape
    fine = (sites, nrhs, 2, arrays[-1].shape[-1])
    return pl.pallas_call(
        finish_kernel,
        in_specs=[VM] * 8,
        out_specs=[HBM, HBM],
        out_shape=[jax.ShapeDtypeStruct(fine, BF16), jax.ShapeDtypeStruct((sites, nrhs, wide), F32)],
        scratch_shapes=[
            pltpu.VMEM((wide, wide), F32),
            pltpu.VMEM((sites, 2, 2 * nrhs, wide), F32),
            pltpu.VMEM(fine, BF16),
            pltpu.VMEM((sites, nrhs, wide), F32),
            pltpu.SemaphoreType.DMA((sites // EACH,)),
            pltpu.SemaphoreType.DMA,
        ],
        compiler_params=PARAMS,
        name="finish",
    )(sums, *arrays)


def on_device(fine_residual, near_null, coarse_operator):
    ly, lx, nrhs, _, fine = fine_residual.shape[2:]
    sites = ly * lx
    nvec = near_null.shape[-2]
    wide = 4 * nvec
    field = fine_residual.reshape(sites, nrhs, 2, fine)
    near = near_null.reshape(sites, 2 * nvec, fine)
    oper = coarse_operator.reshape((-1, sites) + coarse_operator.shape[-2:])
    dims = (ly, lx)
    field, near, oper = (pltpu.with_memory_space_constraint(a, pltpu.HBM) for a in (field, near, oper))
    vector = jax.ShapeDtypeStruct((sites, nrhs, wide), F32)
    rounded = jax.ShapeDtypeStruct((sites, nrhs, wide), BF16)
    xy = pltpu.VMEM((sites, 2 * nrhs, wide), BF16)

    r0, h0, l0, near, oper = restrict(field, near, oper)

    planes = exchange(h0)
    part, w1 = pl.pallas_call(
        functools.partial(first_local_kernel, dims),
        in_specs=[VM] * 3,
        out_specs=[VM] * 2,
        out_shape=[vector, vector],
        scratch_shapes=[xy],
        compiler_params=PARAMS,
        name="local_1",
    )(h0, l0, oper)
    v1, h1, l1 = pl.pallas_call(
        halo_kernel,
        in_specs=[VM] * 7,
        out_specs=[VM] * 3,
        out_shape=[vector, rounded, rounded],
        compiler_params=PARAMS,
        name="halo_1",
    )(*planes, part, r0, oper)

    planes = exchange(h1)
    part, w2 = pl.pallas_call(
        functools.partial(later_local_kernel, dims, True),
        in_specs=[VM] * 4,
        out_specs=[VM] * 2,
        out_shape=[vector, vector],
        scratch_shapes=[xy],
        compiler_params=PARAMS,
        name="local_2",
    )(h1, l1, w1, oper)
    v2, h2, l2 = pl.pallas_call(
        halo_kernel,
        in_specs=[VM] * 7,
        out_specs=[VM] * 3,
        out_shape=[vector, rounded, rounded],
        compiler_params=PARAMS,
        name="halo_2",
    )(*planes, part, v1, oper)

    planes = exchange(h2)
    part = pl.pallas_call(
        functools.partial(later_local_kernel, dims, False),
        in_specs=[VM] * 3,
        out_specs=VM,
        out_shape=vector,
        scratch_shapes=[xy],
        compiler_params=PARAMS,
        name="local_3",
    )(h2, l2, oper)
    devices = lax.axis_size("grp") * lax.axis_size("dev")
    v3, sums = pl.pallas_call(
        last_kernel,
        in_specs=[VM] * 11,
        out_specs=[VM] * 2,
        out_shape=[vector, jax.ShapeDtypeStruct((devices, 8, wide), F32)],
        compiler_params=PARAMS,
        name="halo_3",
    )(*planes, part, r0, v1, w1, v2, w2, oper)

    sums = lax.all_to_all(sums, ("grp", "dev"), 0, 0)
    correction, residual = finish(sums, r0, v1, w1, v2, w2, v3, near)
    return correction.reshape(fine_residual.shape), residual.reshape((1, 1, ly, lx, nrhs, wide))


def solution(mesh):
    in_specs = (
        P("grp", "dev", None, None, None, None, None),
        P("grp", "dev", None, None, None, None, None),
        P(None, "dev", None, None, None, None),
    )
    out_specs = (
        P("grp", "dev", None, None, None, None, None),
        P("grp", "dev", None, None, None, None),
    )
    return jax.shard_map(
        on_device, mesh=mesh, in_specs=in_specs, out_specs=out_specs, check_vma=False
    )
```

```python
import functools

import jax
import jax.numpy as jnp
from jax import lax
from jax.experimental import pallas as pl
from jax.experimental.pallas import tpu as pltpu
from jax.sharding import PartitionSpec as P

ITERS = 3
BASIS = 6
SHIFT = 3.0
EACH = 2
WAVE = 2
LIMIT = 16 * 1024 * 1024
F32 = jnp.float32
BF16 = jnp.bfloat16
NT = (((1,), (1,)), ((), ()))
NN = (((1,), (0,)), ((), ()))
VM = pl.BlockSpec(memory_space=pltpu.VMEM)
HBM = pl.BlockSpec(memory_space=pltpu.HBM)
PARAMS = pltpu.CompilerParams(vmem_limit_bytes=LIMIT)


def pairings(count):
    if count % 2:
        ahead = [(i, (i - 1) % count) for i in range(count)]
        return ahead, [(target, source) for source, target in ahead]
    first = [(i, i ^ 1) for i in range(count)]
    second = [(i, (i + 1) % count if i % 2 else (i - 1) % count) for i in range(count)]
    return first, second


def swapped(axis):
    if lax.axis_size(axis) % 2:
        return jnp.bool_(False)
    return lax.rem(lax.axis_index(axis), 2) == 1


def exchange(high):
    z_first, z_second = pairings(lax.axis_size("dev"))
    t_first, t_second = pairings(lax.axis_size("grp"))
    t_two = lax.ppermute(high, "grp", t_second)
    z_two = lax.ppermute(high, "dev", z_second)
    z_one = lax.ppermute(high, "dev", z_first)
    t_one = lax.ppermute(high, "grp", t_first)
    return t_one, t_two, z_one, z_two


def lanes(shape):
    return lax.broadcasted_iota(jnp.int32, shape, len(shape) - 1)


def stacked(vector):
    wide = vector.astype(F32)
    half = wide.shape[-1] // 2
    turned = pltpu.roll(wide, half, 1)
    sign = jnp.where(lanes(wide.shape) < half, 1.0, -1.0)
    return jnp.concatenate([wide * sign, turned], axis=0).astype(BF16)


def halves(value):
    high = value.astype(BF16)
    return high, (value - high.astype(F32)).astype(BF16)


def joined(product, rows):
    return jnp.concatenate([product[:rows], product[rows:]], axis=1)


def restrict_kernel(
    field_hbm, near_hbm, oper_hbm, source_ref, high_ref, low_ref, near_ref, oper_ref, field, prods, sem, oper_sem
):
    sites, nrhs = field.shape[:2]
    middle = field.shape[-1] // 2
    nvec = near_ref.shape[1] // 2
    wide = 4 * nvec
    groups = sem.shape[1]
    each = EACH
    copies = []
    for g in range(groups):
        span = pl.ds(g * each, each)
        pair = (
            pltpu.make_async_copy(field_hbm.at[span], field.at[span], sem.at[0, g]),
            pltpu.make_async_copy(near_hbm.at[span], near_ref.at[span], sem.at[1, g]),
        )
        for copy in pair:
            copy.start()
        copies.append(pair)
    last = pltpu.make_async_copy(oper_hbm.at[lax.axis_index("grp")], oper_ref, oper_sem)
    last.start()
    lane = lanes((nrhs, wide))

    def multiply(s):
        fine = field[s].reshape(2 * nrhs, 2 * middle)
        near = near_ref[s]
        parts = [
            lax.dot_general(
                fine[:, h * middle : (h + 1) * middle],
                near[:, h * middle : (h + 1) * middle],
                NT,
                preferred_element_type=F32,
            )
            for h in range(2)
        ]
        prods[s] = jnp.concatenate(parts, axis=1)

    def arrange(s):
        even = prods[s, pl.ds(0, nrhs, 2), :]
        odd = prods[s, pl.ds(1, nrhs, 2), :]
        real = even + pltpu.roll(odd, wide - nvec, 1)
        imag = odd - pltpu.roll(even, wide - nvec, 1)
        value = jnp.where(
            lane < nvec,
            real,
            jnp.where(
                lane < 2 * nvec,
                pltpu.roll(real, wide - nvec, 1),
                jnp.where(lane < 3 * nvec, pltpu.roll(imag, 2 * nvec, 1), pltpu.roll(imag, nvec, 1)),
            ),
        )
        source_ref[s] = value
        high_ref[s], low_ref[s] = halves(value)

    for g in range(groups + 1):
        if g < groups:
            for copy in copies[g]:
                copy.wait()
            for s in range(g * each, (g + 1) * each):
                multiply(s)
        if g:
            for s in range((g - 1) * each, g * each):
                arrange(s)
    last.wait()


def restrict(field, near, oper):
    sites, nrhs, _, fine = field.shape
    coarse = 2 * near.shape[1]
    return pl.pallas_call(
        restrict_kernel,
        in_specs=[HBM] * 3,
        out_specs=[VM] * 5,
        out_shape=[
            jax.ShapeDtypeStruct((sites, nrhs, coarse), F32),
            jax.ShapeDtypeStruct((sites, nrhs, coarse), BF16),
            jax.ShapeDtypeStruct((sites, nrhs, coarse), BF16),
            jax.ShapeDtypeStruct(near.shape, BF16),
            jax.ShapeDtypeStruct(oper.shape[1:], BF16),
        ],
        scratch_shapes=[
            pltpu.VMEM(field.shape, BF16),
            pltpu.VMEM((sites, 2 * nrhs, coarse), F32),
            pltpu.SemaphoreType.DMA((2, sites // EACH)),
            pltpu.SemaphoreType.DMA,
        ],
        compiler_params=PARAMS,
        name="restrict",
    )(field, near, oper)


def neighbours(s, ly, lx):
    y, x = s // lx, s % lx
    return [((y + 1) % ly) * lx + x, ((y - 1) % ly) * lx + x, y * lx + (x + 1) % lx, y * lx + (x - 1) % lx]


def local_product(s, dims, blocks, xy, extra):
    rows = xy.shape[1]
    wide = xy.shape[2]
    centre = lax.dot_general(
        jnp.concatenate([xy[s]] + [stacked(e) for e in extra], axis=0),
        blocks[:, :wide],
        NT,
        preferred_element_type=F32,
    )
    sides = lax.dot_general(
        jnp.concatenate([xy[j] for j in neighbours(s, *dims)], axis=1),
        blocks[:, 5 * wide :],
        NT,
        preferred_element_type=F32,
    )
    total = centre[:rows] + sides
    return total, [centre[(i + 1) * rows : (i + 2) * rows] for i in range(len(extra))]


def first_local_kernel(dims, high, low, oper_ref, part_ref, rest_ref, xy):
    sites = xy.shape[0]
    rows = high.shape[1]
    for s in range(sites):
        xy[s] = stacked(high[s])
    for s in range(sites):
        total, extra = local_product(s, dims, oper_ref[s], xy, [low[s]])
        part_ref[s] = joined(total, rows)
        rest_ref[s] = joined(extra[0], rows)


def second_local_kernel(dims, high, low, rest, oper_ref, part_ref, rest_ref, xy):
    sites = xy.shape[0]
    rows = high.shape[1]
    for s in range(sites):
        xy[s] = stacked(high[s])
    for s in range(sites):
        total, more = local_product(s, dims, oper_ref[s], xy, [low[s], rest[s]])
        part_ref[s] = joined(total + more[0], rows)
        rest_ref[s] = joined(more[1], rows)


def third_local_kernel(dims, high, low, r0, v1, w1, v2, w2, oper_ref, part_ref, sums_ref, xy):
    sites = xy.shape[0]
    rows = high.shape[1]
    for s in range(sites):
        xy[s] = stacked(high[s])
    for s in range(sites):
        total, more = local_product(s, dims, oper_ref[s], xy, [low[s]])
        part_ref[s] = joined(total + more[0], rows)
    basis = [r0, v1, w1, v2, w2]
    sums_ref[...] = inner_sums(basis, {k: i for k, i in slots(BASIS).items() if k[1] < BASIS - 1})


def halo_value(s, flips, planes, part, before, oper_ref):
    rows, wide = part.shape[1], part.shape[2]
    cols = []
    for flip, (one, two) in zip(flips, planes):
        a, b = one[s].astype(F32), two[s].astype(F32)
        cols.append(stacked(jnp.where(flip, b, a)))
        cols.append(stacked(jnp.where(flip, a, b)))
    product = lax.dot_general(
        jnp.concatenate(cols, axis=1), oper_ref[s, :, wide : 5 * wide], NT, preferred_element_type=F32
    )
    return part[s] + joined(product, rows) - SHIFT * before[s]


def halo_kernel(t_one, t_two, z_one, z_two, part, before, oper_ref, value_ref, high_ref, low_ref):
    flips = (swapped("grp"), swapped("dev"))
    for s in range(part.shape[0]):
        value = halo_value(s, flips, ((t_one, t_two), (z_one, z_two)), part, before, oper_ref)
        value_ref[s] = value
        high_ref[s], low_ref[s] = halves(value)


def slots(count):
    table = {}
    for i in range(count):
        for j in range(i, count):
            table[(i, j, 0)] = len(table)
            if j > i:
                table[(i, j, 1)] = len(table)
    return table


def inner_sums(basis, table):
    sites, rows, wide = basis[0].shape
    half = wide // 2
    total = {key: jnp.zeros((rows, wide), F32) for key in table}
    for s in range(sites):
        plain = [b[s] for b in basis]
        turned = {j: pltpu.roll(plain[j], half, 1) for j in sorted({k[1] for k in table if k[2]})}
        for i, j, imaginary in table:
            total[(i, j, imaginary)] += plain[i] * (turned[j] if imaginary else plain[j])
    lane = lanes((rows, wide))
    sign = jnp.where(lane < half, 1.0, -1.0)
    packed = jnp.zeros((rows, wide), F32)
    for key, slot in table.items():
        value = total[key] * sign if key[2] else total[key]
        packed = jnp.where(lane == slot, jnp.sum(value, axis=1, keepdims=True), packed)
    return packed


def last_kernel(t_one, t_two, z_one, z_two, part, r0, v1, w1, v2, w2, early, oper_ref, v3, sums_ref):
    flips = (swapped("grp"), swapped("dev"))
    sites, rows, wide = part.shape
    for s in range(sites):
        v3[s] = halo_value(s, flips, ((t_one, t_two), (z_one, z_two)), part, v2, oper_ref)
    table = slots(BASIS)
    late = inner_sums([r0, v1, w1, v2, w2, v3], {k: i for k, i in table.items() if k[1] == BASIS - 1})
    packed = early[...] + late
    square = jnp.concatenate([packed, jnp.zeros((wide - rows, wide), F32)], axis=0).T
    dense = jnp.zeros((8, wide), F32)
    for group in range(-(-len(table) // 8)):
        piece = square[8 * group : 8 * group + 8]
        dense = dense + (pltpu.roll(piece, rows * group, 1) if group else piece)
    for d in range(sums_ref.shape[0]):
        sums_ref[d] = dense


def times(a, b):
    return (a[0] * b[0] - a[1] * b[1], a[0] * b[1] + a[1] * b[0])


def plus(a, b):
    return (a[0] + b[0], a[1] + b[1])


def minus(a, b):
    return (a[0] - b[0], a[1] - b[1])


def over(a, b):
    return (a[0] / b, a[1] / b)


def combine(a, b, op):
    out = []
    for x, y in zip(a, b):
        if y is None:
            out.append(x)
        elif x is None:
            out.append(y if op is plus else (-y[0], -y[1]))
        else:
            out.append(op(x, y))
    return out


def scale(c, a):
    return [None if x is None else times(c, x) for x in a]


def recurrences(gram, one):
    zero = jnp.zeros_like(one)

    def entry(i, j):
        if i == j:
            return (gram[(i, i, 0)], zero)
        if i < j:
            return (gram[(i, j, 0)], gram[(i, j, 1)])
        return (gram[(j, i, 0)], -gram[(j, i, 1)])

    count = BASIS

    def lower(a):
        out = []
        for i in range(count):
            total = (zero, zero)
            for j in range(count):
                if a[j] is not None:
                    total = plus(total, times(entry(i, j), a[j]))
            out.append(total)
        return out

    def inner(a, lowered):
        total = (zero, zero)
        for x, y in zip(a, lowered):
            if x is not None:
                total = plus(total, times((x[0], -x[1]), y))
        return total

    def apply(a, rounded):
        out = [None] * count
        shift = lambda x: (SHIFT * x[0], SHIFT * x[1])
        for source, target in ((0, 1), (1, 3), (3, 5)):
            if a[source] is not None:
                out = combine(out, [shift(a[source]) if k == source else None for k in range(count)], plus)
                out = combine(out, [a[source] if k == target else None for k in range(count)], plus)
        if a[0] is not None and not rounded:
            out = combine(out, [a[0] if k == 2 else None for k in range(count)], plus)
        if a[2] is not None:
            out = combine(out, [a[2] if k == 4 else None for k in range(count)], plus)
        return out

    residual = [(one, zero)] + [None] * (count - 1)
    answer = [None] * count
    directions, images, lows, curvatures = [], [], [], []
    for iteration in range(ITERS):
        direction = residual
        image = apply(direction, iteration == 0)
        factors = [over(inner(image, low), c) for low, c in zip(lows, curvatures)]
        factors = [(f[0], -f[1]) for f in factors]
        for f, p, q in zip(factors, directions, images):
            image = combine(image, scale(f, q), minus)
            direction = combine(direction, scale(f, p), minus)
        low = lower(image)
        curvature = inner(image, low)[0]
        along = inner(residual, low)
        step = over((along[0], -along[1]), curvature)
        answer = combine(answer, scale(step, direction), plus)
        residual = combine(residual, scale(step, image), minus)
        directions.append(direction)
        images.append(image)
        lows.append(low)
        curvatures.append(curvature)
    return answer, residual


def finish_kernel(sums, r0, v1, w1, v2, w2, v3, near, fine_hbm, resid_hbm, coef, mixed, fine, resid, sem, resid_sem):
    sites, rows, wide = r0.shape
    half = wide // 2
    quarter = half // 2
    middle = near.shape[-1] // 2
    dense = sums[0]
    for d in range(1, sums.shape[0]):
        dense = dense + sums[d]
    basis = [r0, v1, w1, v2, w2, v3]
    table = slots(BASIS)
    turned = [dense if g == 0 else pltpu.roll(dense, wide - rows * g, 1) for g in range(-(-len(table) // 8))]
    gram = {key: turned[slot // 8][slot % 8 : slot % 8 + 1] for key, slot in table.items()}
    answer, residual = recurrences(gram, jnp.ones((1, wide), F32))
    entries = []
    for which, coords in ((0, answer), (1, residual)):
        for index, value in enumerate(coords):
            if value is not None:
                entries.append((which, index, value))
    coef[...] = jnp.zeros_like(coef)
    for e, (_, _, value) in enumerate(entries):
        coef[2 * e : 2 * e + 1] = value[0]
        coef[2 * e + 1 : 2 * e + 2] = value[1]
    columns = coef[...].T[:rows]
    sign = jnp.where(lanes((8, wide)) < half, -1.0, 1.0)
    spread = [
        (
            which,
            index,
            jnp.broadcast_to(columns[:, 2 * e : 2 * e + 1], (rows, wide)),
            jnp.broadcast_to(columns[:, 2 * e + 1 : 2 * e + 2], (rows, wide)),
        )
        for e, (which, index, _) in enumerate(entries)
    ]
    low = lanes((8, wide)) < quarter

    def combined(s, block):
        span = slice(8 * block, 8 * block + 8)
        plain = [b[s, span, :] for b in basis]
        out = []
        for which in range(2):
            terms = [(re[span] * plain[i], im[span] * plain[i]) for w, i, re, im in spread if w == which]
            re, im = functools.reduce(plus, terms)
            out.append(re + pltpu.roll(im, half, 1) * sign)
        resid[s, span, :] = out[1]
        x = out[0].astype(BF16).astype(F32)
        by1 = pltpu.roll(x, wide - quarter, 1)
        by2 = pltpu.roll(x, half, 1)
        by3 = pltpu.roll(x, quarter, 1)
        even, odd = pl.ds(16 * block, 8, 2), pl.ds(16 * block + 1, 8, 2)
        mixed[s, 0, even, :] = jnp.where(low, x, -by1)
        mixed[s, 0, odd, :] = jnp.where(low, by2, by3)
        mixed[s, 1, even, :] = jnp.where(low, by1, -by2)
        mixed[s, 1, odd, :] = jnp.where(low, by3, x)

    def prolonged(s):
        for h in range(2):
            cols = slice(h * middle, (h + 1) * middle)
            product = lax.dot_general(
                mixed[s, h, :, :half].astype(BF16), near[s, :, cols], NN, preferred_element_type=F32
            )
            fine[s, :, :, cols] = product.astype(BF16).reshape(rows, 2, middle)

    groups = sem.shape[0]
    copies = []
    for g in range(groups + 1):
        if g < groups and g % WAVE == 0:
            for block in range(rows // 8):
                for s in range(g * EACH, (g + WAVE) * EACH):
                    combined(s, block)
        if g == groups - WAVE:
            copies.append(pltpu.make_async_copy(resid, resid_hbm, resid_sem))
            copies[-1].start()
        if g:
            span = pl.ds((g - 1) * EACH, EACH)
            for s in range((g - 1) * EACH, g * EACH):
                prolonged(s)
            copies.append(pltpu.make_async_copy(fine.at[span], fine_hbm.at[span], sem.at[g - 1]))
            copies[-1].start()
    for copy in copies:
        copy.wait()


def finish(sums, *arrays):
    sites, nrhs, wide = arrays[0].shape
    fine = (sites, nrhs, 2, arrays[-1].shape[-1])
    return pl.pallas_call(
        finish_kernel,
        in_specs=[VM] * 8,
        out_specs=[HBM, HBM],
        out_shape=[jax.ShapeDtypeStruct(fine, BF16), jax.ShapeDtypeStruct((sites, nrhs, wide), F32)],
        scratch_shapes=[
            pltpu.VMEM((wide, wide), F32),
            pltpu.VMEM((sites, 2, 2 * nrhs, wide), F32),
            pltpu.VMEM(fine, BF16),
            pltpu.VMEM((sites, nrhs, wide), F32),
            pltpu.SemaphoreType.DMA((sites // EACH,)),
            pltpu.SemaphoreType.DMA,
        ],
        compiler_params=PARAMS,
        name="finish",
    )(sums, *arrays)


def on_device(fine_residual, near_null, coarse_operator):
    ly, lx, nrhs, _, fine = fine_residual.shape[2:]
    sites = ly * lx
    nvec = near_null.shape[-2]
    wide = 4 * nvec
    field = fine_residual.reshape(sites, nrhs, 2, fine)
    near = near_null.reshape(sites, 2 * nvec, fine)
    oper = coarse_operator.reshape((-1, sites) + coarse_operator.shape[-2:])
    dims = (ly, lx)
    field, near, oper = (pltpu.with_memory_space_constraint(a, pltpu.HBM) for a in (field, near, oper))
    vector = jax.ShapeDtypeStruct((sites, nrhs, wide), F32)
    rounded = jax.ShapeDtypeStruct((sites, nrhs, wide), BF16)
    xy = pltpu.VMEM((sites, 2 * nrhs, wide), BF16)

    r0, h0, l0, near, oper = restrict(field, near, oper)

    planes = exchange(h0)
    part, w1 = pl.pallas_call(
        functools.partial(first_local_kernel, dims),
        in_specs=[VM] * 3,
        out_specs=[VM] * 2,
        out_shape=[vector, vector],
        scratch_shapes=[xy],
        compiler_params=PARAMS,
        name="local_1",
    )(h0, l0, oper)
    v1, h1, l1 = pl.pallas_call(
        halo_kernel,
        in_specs=[VM] * 7,
        out_specs=[VM] * 3,
        out_shape=[vector, rounded, rounded],
        compiler_params=PARAMS,
        name="halo_1",
    )(*planes, part, r0, oper)

    planes = exchange(h1)
    part, w2 = pl.pallas_call(
        functools.partial(second_local_kernel, dims),
        in_specs=[VM] * 4,
        out_specs=[VM] * 2,
        out_shape=[vector, vector],
        scratch_shapes=[xy],
        compiler_params=PARAMS,
        name="local_2",
    )(h1, l1, w1, oper)
    v2, h2, l2 = pl.pallas_call(
        halo_kernel,
        in_specs=[VM] * 7,
        out_specs=[VM] * 3,
        out_shape=[vector, rounded, rounded],
        compiler_params=PARAMS,
        name="halo_2",
    )(*planes, part, v1, oper)

    planes = exchange(h2)
    part, early = pl.pallas_call(
        functools.partial(third_local_kernel, dims),
        in_specs=[VM] * 8,
        out_specs=[VM] * 2,
        out_shape=[vector, jax.ShapeDtypeStruct((nrhs, wide), F32)],
        scratch_shapes=[xy],
        compiler_params=PARAMS,
        name="local_3",
    )(h2, l2, r0, v1, w1, v2, w2, oper)
    devices = lax.axis_size("grp") * lax.axis_size("dev")
    v3, sums = pl.pallas_call(
        last_kernel,
        in_specs=[VM] * 12,
        out_specs=[VM] * 2,
        out_shape=[vector, jax.ShapeDtypeStruct((devices, 8, wide), F32)],
        compiler_params=PARAMS,
        name="halo_3",
    )(*planes, part, r0, v1, w1, v2, w2, early, oper)

    sums = lax.all_to_all(sums, ("grp", "dev"), 0, 0)
    correction, residual = finish(sums, r0, v1, w1, v2, w2, v3, near)
    return correction.reshape(fine_residual.shape), residual.reshape((1, 1, ly, lx, nrhs, wide))


def solution(mesh):
    in_specs = (
        P("grp", "dev", None, None, None, None, None),
        P("grp", "dev", None, None, None, None, None),
        P(None, "dev", None, None, None, None),
    )
    out_specs = (
        P("grp", "dev", None, None, None, None, None),
        P("grp", "dev", None, None, None, None),
    )
    return jax.shard_map(
        on_device, mesh=mesh, in_specs=in_specs, out_specs=out_specs, check_vma=False
    )
```

```python
import functools

import jax
import jax.numpy as jnp
from jax import lax
from jax.experimental import pallas as pl
from jax.experimental.pallas import tpu as pltpu
from jax.sharding import PartitionSpec as P

ITERS = 3
BASIS = 6
SHIFT = 3.0
EACH = 2
WAVE = 2
LIMIT = 16 * 1024 * 1024
F32 = jnp.float32
BF16 = jnp.bfloat16
NT = (((1,), (1,)), ((), ()))
NN = (((1,), (0,)), ((), ()))
VM = pl.BlockSpec(memory_space=pltpu.VMEM)
HBM = pl.BlockSpec(memory_space=pltpu.HBM)
PARAMS = pltpu.CompilerParams(vmem_limit_bytes=LIMIT)


def pairings(count):
    if count % 2:
        ahead = [(i, (i - 1) % count) for i in range(count)]
        return ahead, [(target, source) for source, target in ahead]
    first = [(i, i ^ 1) for i in range(count)]
    second = [(i, (i + 1) % count if i % 2 else (i - 1) % count) for i in range(count)]
    return first, second


def swapped(axis):
    if lax.axis_size(axis) % 2:
        return jnp.bool_(False)
    return lax.rem(lax.axis_index(axis), 2) == 1


def exchange(high):
    z_first, z_second = pairings(lax.axis_size("dev"))
    t_first, t_second = pairings(lax.axis_size("grp"))
    t_two = lax.ppermute(high, "grp", t_second)
    z_two = lax.ppermute(high, "dev", z_second)
    z_one = lax.ppermute(high, "dev", z_first)
    t_one = lax.ppermute(high, "grp", t_first)
    return t_one, t_two, z_one, z_two


def lanes(shape):
    return lax.broadcasted_iota(jnp.int32, shape, len(shape) - 1)


def stacked(vector):
    wide = vector.astype(F32)
    half = wide.shape[-1] // 2
    turned = pltpu.roll(wide, half, 1)
    sign = jnp.where(lanes(wide.shape) < half, 1.0, -1.0)
    return jnp.concatenate([wide * sign, turned], axis=0).astype(BF16)


def halves(value):
    high = value.astype(BF16)
    return high, (value - high.astype(F32)).astype(BF16)


def joined(product, rows):
    return jnp.concatenate([product[:rows], product[rows:]], axis=1)


def batches(sites):
    return [(s, EACH) for s in range(0, sites, EACH)]


def restrict_kernel(
    field_hbm, near_hbm, source_ref, high_ref, low_ref, near_ref, field, prods, sem
):
    sites, nrhs = field.shape[:2]
    middle = field.shape[-1] // 2
    nvec = near_ref.shape[1] // 2
    wide = 4 * nvec
    groups = batches(sites)
    copies = []
    for g, (first, count) in enumerate(groups):
        span = pl.ds(first, count)
        pair = (
            pltpu.make_async_copy(field_hbm.at[span], field.at[span], sem.at[0, g]),
            pltpu.make_async_copy(near_hbm.at[span], near_ref.at[span], sem.at[1, g]),
        )
        for copy in pair:
            copy.start()
        copies.append(pair)
    lane = lanes((nrhs, wide))

    def multiply(s):
        fine = field[s].reshape(2 * nrhs, 2 * middle)
        near = near_ref[s]
        parts = [
            lax.dot_general(
                fine[:, h * middle : (h + 1) * middle],
                near[:, h * middle : (h + 1) * middle],
                NT,
                preferred_element_type=F32,
            )
            for h in range(2)
        ]
        prods[s] = jnp.concatenate(parts, axis=1)

    def arrange(s):
        even = prods[s, pl.ds(0, nrhs, 2), :]
        odd = prods[s, pl.ds(1, nrhs, 2), :]
        real = even + pltpu.roll(odd, wide - nvec, 1)
        imag = odd - pltpu.roll(even, wide - nvec, 1)
        value = jnp.where(
            lane < nvec,
            real,
            jnp.where(
                lane < 2 * nvec,
                pltpu.roll(real, wide - nvec, 1),
                jnp.where(lane < 3 * nvec, pltpu.roll(imag, 2 * nvec, 1), pltpu.roll(imag, nvec, 1)),
            ),
        )
        source_ref[s] = value
        high_ref[s], low_ref[s] = halves(value)

    for g in range(len(groups) + 1):
        if g < len(groups):
            for copy in copies[g]:
                copy.wait()
            for s in range(groups[g][0], sum(groups[g])):
                multiply(s)
        if g:
            for s in range(groups[g - 1][0], sum(groups[g - 1])):
                arrange(s)


def restrict(field, near):
    sites, nrhs, _, fine = field.shape
    coarse = 2 * near.shape[1]
    return pl.pallas_call(
        restrict_kernel,
        in_specs=[HBM] * 2,
        out_specs=[VM] * 4,
        out_shape=[
            jax.ShapeDtypeStruct((sites, nrhs, coarse), F32),
            jax.ShapeDtypeStruct((sites, nrhs, coarse), BF16),
            jax.ShapeDtypeStruct((sites, nrhs, coarse), BF16),
            jax.ShapeDtypeStruct(near.shape, BF16),
        ],
        scratch_shapes=[
            pltpu.VMEM(field.shape, BF16),
            pltpu.VMEM((sites, 2 * nrhs, coarse), F32),
            pltpu.SemaphoreType.DMA((2, len(batches(sites)))),
        ],
        compiler_params=PARAMS,
        name="restrict",
    )(field, near)


def neighbours(s, ly, lx):
    y, x = s // lx, s % lx
    return [((y + 1) % ly) * lx + x, ((y - 1) % ly) * lx + x, y * lx + (x + 1) % lx, y * lx + (x - 1) % lx]


def local_product(s, dims, blocks, xy, extra):
    rows = xy.shape[1]
    wide = xy.shape[2]
    centre = lax.dot_general(
        jnp.concatenate([xy[s]] + [stacked(e) for e in extra], axis=0),
        blocks[:, :wide],
        NT,
        preferred_element_type=F32,
    )
    sides = lax.dot_general(
        jnp.concatenate([xy[j] for j in neighbours(s, *dims)], axis=1),
        blocks[:, 5 * wide :],
        NT,
        preferred_element_type=F32,
    )
    total = centre[:rows] + sides
    return total, [centre[(i + 1) * rows : (i + 2) * rows] for i in range(len(extra))]


def first_local_kernel(dims, high, low, oper_hbm, part_ref, rest_ref, oper_ref, xy, sem):
    copy = pltpu.make_async_copy(oper_hbm.at[lax.axis_index("grp")], oper_ref, sem)
    copy.start()
    sites = xy.shape[0]
    rows = high.shape[1]
    for s in range(sites):
        xy[s] = stacked(high[s])
    copy.wait()
    for s in range(sites):
        total, extra = local_product(s, dims, oper_ref[s], xy, [low[s]])
        part_ref[s] = joined(total, rows)
        rest_ref[s] = joined(extra[0], rows)


def second_local_kernel(dims, high, low, rest, oper_ref, part_ref, rest_ref, xy):
    sites = xy.shape[0]
    rows = high.shape[1]
    for s in range(sites):
        xy[s] = stacked(high[s])
    for s in range(sites):
        total, more = local_product(s, dims, oper_ref[s], xy, [low[s], rest[s]])
        part_ref[s] = joined(total + more[0], rows)
        rest_ref[s] = joined(more[1], rows)


def third_local_kernel(dims, high, low, r0, v1, w1, v2, w2, oper_ref, part_ref, sums_ref, xy):
    sites = xy.shape[0]
    rows = high.shape[1]
    for s in range(sites):
        xy[s] = stacked(high[s])
    for s in range(sites):
        total, more = local_product(s, dims, oper_ref[s], xy, [low[s]])
        part_ref[s] = joined(total + more[0], rows)
    basis = [r0, v1, w1, v2, w2]
    sums_ref[...] = inner_sums(basis, {k: i for k, i in slots(BASIS).items() if k[1] < BASIS - 1})


def halo_value(s, flips, planes, part, before, oper_ref):
    rows, wide = part.shape[1], part.shape[2]
    cols = []
    for flip, (one, two) in zip(flips, planes):
        a, b = one[s].astype(F32), two[s].astype(F32)
        cols.append(stacked(jnp.where(flip, b, a)))
        cols.append(stacked(jnp.where(flip, a, b)))
    product = lax.dot_general(
        jnp.concatenate(cols, axis=1), oper_ref[s, :, wide : 5 * wide], NT, preferred_element_type=F32
    )
    return part[s] + joined(product, rows) - SHIFT * before[s]


def halo_kernel(t_one, t_two, z_one, z_two, part, before, oper_ref, value_ref, high_ref, low_ref):
    flips = (swapped("grp"), swapped("dev"))
    for s in range(part.shape[0]):
        value = halo_value(s, flips, ((t_one, t_two), (z_one, z_two)), part, before, oper_ref)
        value_ref[s] = value
        high_ref[s], low_ref[s] = halves(value)


def slots(count):
    table = {}
    for i in range(count):
        for j in range(i, count):
            table[(i, j, 0)] = len(table)
            if j > i:
                table[(i, j, 1)] = len(table)
    return table


def inner_sums(basis, table):
    sites, rows, wide = basis[0].shape
    half = wide // 2
    total = {key: jnp.zeros((rows, wide), F32) for key in table}
    for s in range(sites):
        plain = [b[s] for b in basis]
        turned = {j: pltpu.roll(plain[j], half, 1) for j in sorted({k[1] for k in table if k[2]})}
        for i, j, imaginary in table:
            total[(i, j, imaginary)] += plain[i] * (turned[j] if imaginary else plain[j])
    lane = lanes((rows, wide))
    sign = jnp.where(lane < half, 1.0, -1.0)
    packed = jnp.zeros((rows, wide), F32)
    for key, slot in table.items():
        value = total[key] * sign if key[2] else total[key]
        packed = jnp.where(lane == slot, jnp.sum(value, axis=1, keepdims=True), packed)
    return packed


def last_kernel(t_one, t_two, z_one, z_two, part, r0, v1, w1, v2, w2, early, oper_ref, v3, sums_ref):
    flips = (swapped("grp"), swapped("dev"))
    sites, rows, wide = part.shape
    for s in range(sites):
        v3[s] = halo_value(s, flips, ((t_one, t_two), (z_one, z_two)), part, v2, oper_ref)
    table = slots(BASIS)
    late = inner_sums([r0, v1, w1, v2, w2, v3], {k: i for k, i in table.items() if k[1] == BASIS - 1})
    packed = early[...] + late
    square = packed.T
    groups = -(-len(table) // 8)
    pieces = [square[8 * group : 8 * group + 8] for group in range(groups)]
    dense = jnp.concatenate(pieces + [jnp.zeros((8, wide - rows * groups), F32)], axis=1)
    for d in range(sums_ref.shape[0]):
        sums_ref[d] = dense


def times(a, b):
    return (a[0] * b[0] - a[1] * b[1], a[0] * b[1] + a[1] * b[0])


def plus(a, b):
    return (a[0] + b[0], a[1] + b[1])


def minus(a, b):
    return (a[0] - b[0], a[1] - b[1])


def over(a, b):
    return (a[0] / b, a[1] / b)


def combine(a, b, op):
    out = []
    for x, y in zip(a, b):
        if y is None:
            out.append(x)
        elif x is None:
            out.append(y if op is plus else (-y[0], -y[1]))
        else:
            out.append(op(x, y))
    return out


def scale(c, a):
    return [None if x is None else times(c, x) for x in a]


def recurrences(gram, one):
    zero = jnp.zeros_like(one)

    def entry(i, j):
        if i == j:
            return (gram[(i, i, 0)], zero)
        if i < j:
            return (gram[(i, j, 0)], gram[(i, j, 1)])
        return (gram[(j, i, 0)], -gram[(j, i, 1)])

    count = BASIS

    def lower(a):
        out = []
        for i in range(count):
            total = (zero, zero)
            for j in range(count):
                if a[j] is not None:
                    total = plus(total, times(entry(i, j), a[j]))
            out.append(total)
        return out

    def inner(a, lowered):
        total = (zero, zero)
        for x, y in zip(a, lowered):
            if x is not None:
                total = plus(total, times((x[0], -x[1]), y))
        return total

    def apply(a, rounded):
        out = [None] * count
        shift = lambda x: (SHIFT * x[0], SHIFT * x[1])
        for source, target in ((0, 1), (1, 3), (3, 5)):
            if a[source] is not None:
                out = combine(out, [shift(a[source]) if k == source else None for k in range(count)], plus)
                out = combine(out, [a[source] if k == target else None for k in range(count)], plus)
        if a[0] is not None and not rounded:
            out = combine(out, [a[0] if k == 2 else None for k in range(count)], plus)
        if a[2] is not None:
            out = combine(out, [a[2] if k == 4 else None for k in range(count)], plus)
        return out

    residual = [(one, zero)] + [None] * (count - 1)
    answer = [None] * count
    directions, images, lows, curvatures = [], [], [], []
    for iteration in range(ITERS):
        direction = residual
        image = apply(direction, iteration == 0)
        factors = [over(inner(image, low), c) for low, c in zip(lows, curvatures)]
        factors = [(f[0], -f[1]) for f in factors]
        for f, p, q in zip(factors, directions, images):
            image = combine(image, scale(f, q), minus)
            direction = combine(direction, scale(f, p), minus)
        low = lower(image)
        curvature = inner(image, low)[0]
        along = inner(residual, low)
        step = over((along[0], -along[1]), curvature)
        answer = combine(answer, scale(step, direction), plus)
        residual = combine(residual, scale(step, image), minus)
        directions.append(direction)
        images.append(image)
        lows.append(low)
        curvatures.append(curvature)
    return answer, residual


def finish_kernel(sums, r0, v1, w1, v2, w2, v3, near, fine_hbm, resid_hbm, coef, mixed, fine, resid, sem, resid_sem):
    sites, rows, wide = r0.shape
    half = wide // 2
    quarter = half // 2
    middle = near.shape[-1] // 2
    dense = sums[0]
    for d in range(1, sums.shape[0]):
        dense = dense + sums[d]
    basis = [r0, v1, w1, v2, w2, v3]
    table = slots(BASIS)
    turned = [dense if g == 0 else pltpu.roll(dense, wide - rows * g, 1) for g in range(-(-len(table) // 8))]
    gram = {key: turned[slot // 8][slot % 8 : slot % 8 + 1] for key, slot in table.items()}
    answer, residual = recurrences(gram, jnp.ones((1, wide), F32))
    entries = []
    for which, coords in ((0, answer), (1, residual)):
        for index, value in enumerate(coords):
            if value is not None:
                entries.append((which, index, value))
    coef[...] = jnp.zeros_like(coef)
    for e, (_, _, value) in enumerate(entries):
        coef[2 * e : 2 * e + 1] = value[0]
        coef[2 * e + 1 : 2 * e + 2] = value[1]
    columns = coef[...].T[:rows]
    sign = jnp.where(lanes((8, wide)) < half, -1.0, 1.0)
    spread = [
        (
            which,
            index,
            jnp.broadcast_to(columns[:, 2 * e : 2 * e + 1], (rows, wide)),
            jnp.broadcast_to(columns[:, 2 * e + 1 : 2 * e + 2], (rows, wide)),
        )
        for e, (which, index, _) in enumerate(entries)
    ]
    low = lanes((8, wide)) < quarter

    def combined(s, block):
        span = slice(8 * block, 8 * block + 8)
        plain = [b[s, span, :] for b in basis]
        out = []
        for which in range(2):
            terms = [(re[span] * plain[i], im[span] * plain[i]) for w, i, re, im in spread if w == which]
            re, im = functools.reduce(plus, terms)
            out.append(re + pltpu.roll(im, half, 1) * sign)
        resid[s, span, :] = out[1]
        x = out[0].astype(BF16).astype(F32)
        by1 = pltpu.roll(x, wide - quarter, 1)
        by2 = pltpu.roll(x, half, 1)
        by3 = pltpu.roll(x, quarter, 1)
        even, odd = pl.ds(16 * block, 8, 2), pl.ds(16 * block + 1, 8, 2)
        mixed[s, 0, even, :] = jnp.where(low, x, -by1)
        mixed[s, 0, odd, :] = jnp.where(low, by2, by3)
        mixed[s, 1, even, :] = jnp.where(low, by1, -by2)
        mixed[s, 1, odd, :] = jnp.where(low, by3, x)

    def prolonged(s):
        for h in range(2):
            cols = slice(h * middle, (h + 1) * middle)
            product = lax.dot_general(
                mixed[s, h, :, :half].astype(BF16), near[s, :, cols], NN, preferred_element_type=F32
            )
            fine[s, :, :, cols] = product.astype(BF16).reshape(rows, 2, middle)

    groups = sem.shape[0]
    copies = []
    for g in range(groups + 1):
        if g < groups and g % WAVE == 0:
            for block in range(rows // 8):
                for s in range(g * EACH, (g + WAVE) * EACH):
                    combined(s, block)
        if g == groups - WAVE:
            copies.append(pltpu.make_async_copy(resid, resid_hbm, resid_sem))
            copies[-1].start()
        if g:
            span = pl.ds((g - 1) * EACH, EACH)
            for s in range((g - 1) * EACH, g * EACH):
                prolonged(s)
            copies.append(pltpu.make_async_copy(fine.at[span], fine_hbm.at[span], sem.at[g - 1]))
            copies[-1].start()
    for copy in copies:
        copy.wait()


def finish(sums, *arrays):
    sites, nrhs, wide = arrays[0].shape
    fine = (sites, nrhs, 2, arrays[-1].shape[-1])
    return pl.pallas_call(
        finish_kernel,
        in_specs=[VM] * 8,
        out_specs=[HBM, HBM],
        out_shape=[jax.ShapeDtypeStruct(fine, BF16), jax.ShapeDtypeStruct((sites, nrhs, wide), F32)],
        scratch_shapes=[
            pltpu.VMEM((wide, wide), F32),
            pltpu.VMEM((sites, 2, 2 * nrhs, wide), F32),
            pltpu.VMEM(fine, BF16),
            pltpu.VMEM((sites, nrhs, wide), F32),
            pltpu.SemaphoreType.DMA((sites // EACH,)),
            pltpu.SemaphoreType.DMA,
        ],
        compiler_params=PARAMS,
        name="finish",
    )(sums, *arrays)


def on_device(fine_residual, near_null, coarse_operator):
    ly, lx, nrhs, _, fine = fine_residual.shape[2:]
    sites = ly * lx
    nvec = near_null.shape[-2]
    wide = 4 * nvec
    field = fine_residual.reshape(sites, nrhs, 2, fine)
    near = near_null.reshape(sites, 2 * nvec, fine)
    oper = coarse_operator.reshape((-1, sites) + coarse_operator.shape[-2:])
    dims = (ly, lx)
    field, near, oper = (pltpu.with_memory_space_constraint(a, pltpu.HBM) for a in (field, near, oper))
    vector = jax.ShapeDtypeStruct((sites, nrhs, wide), F32)
    rounded = jax.ShapeDtypeStruct((sites, nrhs, wide), BF16)
    xy = pltpu.VMEM((sites, 2 * nrhs, wide), BF16)

    r0, h0, l0, near = restrict(field, near)

    planes = exchange(h0)
    part, w1, oper = pl.pallas_call(
        functools.partial(first_local_kernel, dims),
        in_specs=[VM, VM, HBM],
        out_specs=[VM] * 3,
        out_shape=[vector, vector, jax.ShapeDtypeStruct(oper.shape[1:], BF16)],
        scratch_shapes=[xy, pltpu.SemaphoreType.DMA],
        compiler_params=PARAMS,
        name="local_1",
    )(h0, l0, oper)
    v1, h1, l1 = pl.pallas_call(
        halo_kernel,
        in_specs=[VM] * 7,
        out_specs=[VM] * 3,
        out_shape=[vector, rounded, rounded],
        compiler_params=PARAMS,
        name="halo_1",
    )(*planes, part, r0, oper)

    planes = exchange(h1)
    part, w2 = pl.pallas_call(
        functools.partial(second_local_kernel, dims),
        in_specs=[VM] * 4,
        out_specs=[VM] * 2,
        out_shape=[vector, vector],
        scratch_shapes=[xy],
        compiler_params=PARAMS,
        name="local_2",
    )(h1, l1, w1, oper)
    v2, h2, l2 = pl.pallas_call(
        halo_kernel,
        in_specs=[VM] * 7,
        out_specs=[VM] * 3,
        out_shape=[vector, rounded, rounded],
        compiler_params=PARAMS,
        name="halo_2",
    )(*planes, part, v1, oper)

    planes = exchange(h2)
    part, early = pl.pallas_call(
        functools.partial(third_local_kernel, dims),
        in_specs=[VM] * 8,
        out_specs=[VM] * 2,
        out_shape=[vector, jax.ShapeDtypeStruct((nrhs, wide), F32)],
        scratch_shapes=[xy],
        compiler_params=PARAMS,
        name="local_3",
    )(h2, l2, r0, v1, w1, v2, w2, oper)
    devices = lax.axis_size("grp") * lax.axis_size("dev")
    v3, sums = pl.pallas_call(
        last_kernel,
        in_specs=[VM] * 12,
        out_specs=[VM] * 2,
        out_shape=[vector, jax.ShapeDtypeStruct((devices, 8, wide), F32)],
        compiler_params=PARAMS,
        name="halo_3",
    )(*planes, part, r0, v1, w1, v2, w2, early, oper)

    sums = lax.all_to_all(sums, ("grp", "dev"), 0, 0)
    correction, residual = finish(sums, r0, v1, w1, v2, w2, v3, near)
    return correction.reshape(fine_residual.shape), residual.reshape((1, 1, ly, lx, nrhs, wide))


def solution(mesh):
    in_specs = (
        P("grp", "dev", None, None, None, None, None),
        P("grp", "dev", None, None, None, None, None),
        P(None, "dev", None, None, None, None),
    )
    out_specs = (
        P("grp", "dev", None, None, None, None, None),
        P("grp", "dev", None, None, None, None),
    )
    return jax.shard_map(
        on_device, mesh=mesh, in_specs=in_specs, out_specs=out_specs, check_vma=False
    )
```

```python
import functools

import jax
import jax.numpy as jnp
from jax import lax
from jax.experimental import pallas as pl
from jax.experimental.pallas import tpu as pltpu
from jax.sharding import PartitionSpec as P

ITERS = 3
BASIS = 6
SHIFT = 3.0
EACH = 2
WAVE = 2
LIMIT = 16 * 1024 * 1024
F32 = jnp.float32
BF16 = jnp.bfloat16
NT = (((1,), (1,)), ((), ()))
NN = (((1,), (0,)), ((), ()))
VM = pl.BlockSpec(memory_space=pltpu.VMEM)
HBM = pl.BlockSpec(memory_space=pltpu.HBM)
PARAMS = pltpu.CompilerParams(vmem_limit_bytes=LIMIT)


def pairings(count, ring=False):
    if ring or count % 2:
        ahead = [(i, (i - 1) % count) for i in range(count)]
        return ahead, [(target, source) for source, target in ahead]
    first = [(i, i ^ 1) for i in range(count)]
    second = [(i, (i + 1) % count if i % 2 else (i - 1) % count) for i in range(count)]
    return first, second


def swapped(axis):
    if lax.axis_size(axis) % 2:
        return jnp.bool_(False)
    return lax.rem(lax.axis_index(axis), 2) == 1


def exchange(high):
    z_first, z_second = pairings(lax.axis_size("dev"))
    t_first, t_second = pairings(lax.axis_size("grp"), True)
    t_two = lax.ppermute(high, "grp", t_second)
    z_two = lax.ppermute(high, "dev", z_second)
    z_one = lax.ppermute(high, "dev", z_first)
    t_one = lax.ppermute(high, "grp", t_first)
    return t_two, t_one, z_one, z_two


def lanes(shape):
    return lax.broadcasted_iota(jnp.int32, shape, len(shape) - 1)


def stacked(vector):
    wide = vector.astype(F32)
    half = wide.shape[-1] // 2
    turned = pltpu.roll(wide, half, 1)
    sign = jnp.where(lanes(wide.shape) < half, 1.0, -1.0)
    return jnp.concatenate([wide * sign, turned], axis=0).astype(BF16)


def halves(value):
    high = value.astype(BF16)
    return high, (value - high.astype(F32)).astype(BF16)


def joined(product, rows):
    return jnp.concatenate([product[:rows], product[rows:]], axis=1)


def batches(sites):
    return [(s, EACH) for s in range(0, sites, EACH)]


def restrict_kernel(
    field_hbm, near_hbm, source_ref, high_ref, low_ref, near_ref, field, prods, sem
):
    sites, nrhs = field.shape[:2]
    middle = field.shape[-1] // 2
    nvec = near_ref.shape[1] // 2
    wide = 4 * nvec
    groups = batches(sites)
    copies = []
    for g, (first, count) in enumerate(groups):
        span = pl.ds(first, count)
        pair = (
            pltpu.make_async_copy(field_hbm.at[span], field.at[span], sem.at[0, g]),
            pltpu.make_async_copy(near_hbm.at[span], near_ref.at[span], sem.at[1, g]),
        )
        for copy in pair:
            copy.start()
        copies.append(pair)
    lane = lanes((nrhs, wide))

    def multiply(s):
        fine = field[s].reshape(2 * nrhs, 2 * middle)
        near = near_ref[s]
        parts = [
            lax.dot_general(
                fine[:, h * middle : (h + 1) * middle],
                near[:, h * middle : (h + 1) * middle],
                NT,
                preferred_element_type=F32,
            )
            for h in range(2)
        ]
        prods[s] = jnp.concatenate(parts, axis=1)

    def arrange(s):
        even = prods[s, pl.ds(0, nrhs, 2), :]
        odd = prods[s, pl.ds(1, nrhs, 2), :]
        real = even + pltpu.roll(odd, wide - nvec, 1)
        imag = odd - pltpu.roll(even, wide - nvec, 1)
        value = jnp.where(
            lane < nvec,
            real,
            jnp.where(
                lane < 2 * nvec,
                pltpu.roll(real, wide - nvec, 1),
                jnp.where(lane < 3 * nvec, pltpu.roll(imag, 2 * nvec, 1), pltpu.roll(imag, nvec, 1)),
            ),
        )
        source_ref[s] = value
        high_ref[s], low_ref[s] = halves(value)

    for g in range(len(groups) + 1):
        if g < len(groups):
            for copy in copies[g]:
                copy.wait()
            for s in range(groups[g][0], sum(groups[g])):
                multiply(s)
        if g:
            for s in range(groups[g - 1][0], sum(groups[g - 1])):
                arrange(s)


def restrict(field, near):
    sites, nrhs, _, fine = field.shape
    coarse = 2 * near.shape[1]
    return pl.pallas_call(
        restrict_kernel,
        in_specs=[HBM] * 2,
        out_specs=[VM] * 4,
        out_shape=[
            jax.ShapeDtypeStruct((sites, nrhs, coarse), F32),
            jax.ShapeDtypeStruct((sites, nrhs, coarse), BF16),
            jax.ShapeDtypeStruct((sites, nrhs, coarse), BF16),
            jax.ShapeDtypeStruct(near.shape, BF16),
        ],
        scratch_shapes=[
            pltpu.VMEM(field.shape, BF16),
            pltpu.VMEM((sites, 2 * nrhs, coarse), F32),
            pltpu.SemaphoreType.DMA((2, len(batches(sites)))),
        ],
        compiler_params=PARAMS,
        name="restrict",
    )(field, near)


def neighbours(s, ly, lx):
    y, x = s // lx, s % lx
    return [((y + 1) % ly) * lx + x, ((y - 1) % ly) * lx + x, y * lx + (x + 1) % lx, y * lx + (x - 1) % lx]


def local_product(s, dims, blocks, xy, extra):
    rows = xy.shape[1]
    wide = xy.shape[2]
    centre = lax.dot_general(
        jnp.concatenate([xy[s]] + [stacked(e) for e in extra], axis=0),
        blocks[:, :wide],
        NT,
        preferred_element_type=F32,
    )
    sides = lax.dot_general(
        jnp.concatenate([xy[j] for j in neighbours(s, *dims)], axis=1),
        blocks[:, 5 * wide :],
        NT,
        preferred_element_type=F32,
    )
    total = centre[:rows] + sides
    return total, [centre[(i + 1) * rows : (i + 2) * rows] for i in range(len(extra))]


def first_local_kernel(dims, high, low, oper_hbm, part_ref, rest_ref, oper_ref, xy, sem):
    copy = pltpu.make_async_copy(oper_hbm.at[lax.axis_index("grp")], oper_ref, sem)
    copy.start()
    sites = xy.shape[0]
    rows = high.shape[1]
    for s in range(sites):
        xy[s] = stacked(high[s])
    copy.wait()
    for s in range(sites):
        total, extra = local_product(s, dims, oper_ref[s], xy, [low[s]])
        part_ref[s] = joined(total, rows)
        rest_ref[s] = joined(extra[0], rows)


def second_local_kernel(dims, high, low, rest, oper_ref, part_ref, rest_ref, xy):
    sites = xy.shape[0]
    rows = high.shape[1]
    for s in range(sites):
        xy[s] = stacked(high[s])
    for s in range(sites):
        total, more = local_product(s, dims, oper_ref[s], xy, [low[s], rest[s]])
        part_ref[s] = joined(total + more[0], rows)
        rest_ref[s] = joined(more[1], rows)


def third_local_kernel(dims, high, low, r0, v1, w1, v2, w2, oper_ref, part_ref, sums_ref, xy):
    sites = xy.shape[0]
    rows = high.shape[1]
    for s in range(sites):
        xy[s] = stacked(high[s])
    for s in range(sites):
        total, more = local_product(s, dims, oper_ref[s], xy, [low[s]])
        part_ref[s] = joined(total + more[0], rows)
    basis = [r0, v1, w1, v2, w2]
    sums_ref[...] = inner_sums(basis, {k: i for k, i in slots(BASIS).items() if k[1] < BASIS - 1})


def halo_value(s, flips, planes, part, before, oper_ref):
    rows, wide = part.shape[1], part.shape[2]
    cols = []
    for flip, (one, two) in zip(flips, planes):
        a, b = one[s].astype(F32), two[s].astype(F32)
        cols.append(stacked(jnp.where(flip, b, a)))
        cols.append(stacked(jnp.where(flip, a, b)))
    product = lax.dot_general(
        jnp.concatenate(cols, axis=1), oper_ref[s, :, wide : 5 * wide], NT, preferred_element_type=F32
    )
    return part[s] + joined(product, rows) - SHIFT * before[s]


def halo_kernel(t_two, t_one, z_one, z_two, part, before, oper_ref, value_ref, high_ref, low_ref):
    flips = (jnp.bool_(False), swapped("dev"))
    for s in range(part.shape[0]):
        value = halo_value(s, flips, ((t_one, t_two), (z_one, z_two)), part, before, oper_ref)
        value_ref[s] = value
        high_ref[s], low_ref[s] = halves(value)


def slots(count):
    table = {}
    for i in range(count):
        for j in range(i, count):
            table[(i, j, 0)] = len(table)
            if j > i:
                table[(i, j, 1)] = len(table)
    return table


def inner_sums(basis, table):
    sites, rows, wide = basis[0].shape
    half = wide // 2
    total = {key: jnp.zeros((rows, wide), F32) for key in table}
    for s in range(sites):
        plain = [b[s] for b in basis]
        turned = {j: pltpu.roll(plain[j], half, 1) for j in sorted({k[1] for k in table if k[2]})}
        for i, j, imaginary in table:
            total[(i, j, imaginary)] += plain[i] * (turned[j] if imaginary else plain[j])
    lane = lanes((rows, wide))
    sign = jnp.where(lane < half, 1.0, -1.0)
    packed = jnp.zeros((rows, wide), F32)
    for key, slot in table.items():
        value = total[key] * sign if key[2] else total[key]
        packed = jnp.where(lane == slot, jnp.sum(value, axis=1, keepdims=True), packed)
    return packed


def last_kernel(t_two, t_one, z_one, z_two, part, r0, v1, w1, v2, w2, early, oper_ref, v3, sums_ref):
    flips = (jnp.bool_(False), swapped("dev"))
    sites, rows, wide = part.shape
    for s in range(sites):
        v3[s] = halo_value(s, flips, ((t_one, t_two), (z_one, z_two)), part, v2, oper_ref)
    table = slots(BASIS)
    late = inner_sums([r0, v1, w1, v2, w2, v3], {k: i for k, i in table.items() if k[1] == BASIS - 1})
    packed = early[...] + late
    square = packed.T
    groups = -(-len(table) // 8)
    pieces = [square[8 * group : 8 * group + 8] for group in range(groups)]
    dense = jnp.concatenate(pieces + [jnp.zeros((8, wide - rows * groups), F32)], axis=1)
    for d in range(sums_ref.shape[0]):
        sums_ref[d] = dense


def times(a, b):
    return (a[0] * b[0] - a[1] * b[1], a[0] * b[1] + a[1] * b[0])


def plus(a, b):
    return (a[0] + b[0], a[1] + b[1])


def minus(a, b):
    return (a[0] - b[0], a[1] - b[1])


def over(a, b):
    return (a[0] / b, a[1] / b)


def combine(a, b, op):
    out = []
    for x, y in zip(a, b):
        if y is None:
            out.append(x)
        elif x is None:
            out.append(y if op is plus else (-y[0], -y[1]))
        else:
            out.append(op(x, y))
    return out


def scale(c, a):
    return [None if x is None else times(c, x) for x in a]


def recurrences(gram, one):
    zero = jnp.zeros_like(one)

    def entry(i, j):
        if i == j:
            return (gram[(i, i, 0)], zero)
        if i < j:
            return (gram[(i, j, 0)], gram[(i, j, 1)])
        return (gram[(j, i, 0)], -gram[(j, i, 1)])

    count = BASIS

    def lower(a):
        out = []
        for i in range(count):
            total = (zero, zero)
            for j in range(count):
                if a[j] is not None:
                    total = plus(total, times(entry(i, j), a[j]))
            out.append(total)
        return out

    def inner(a, lowered):
        total = (zero, zero)
        for x, y in zip(a, lowered):
            if x is not None:
                total = plus(total, times((x[0], -x[1]), y))
        return total

    def apply(a, rounded):
        out = [None] * count
        shift = lambda x: (SHIFT * x[0], SHIFT * x[1])
        for source, target in ((0, 1), (1, 3), (3, 5)):
            if a[source] is not None:
                out = combine(out, [shift(a[source]) if k == source else None for k in range(count)], plus)
                out = combine(out, [a[source] if k == target else None for k in range(count)], plus)
        if a[0] is not None and not rounded:
            out = combine(out, [a[0] if k == 2 else None for k in range(count)], plus)
        if a[2] is not None:
            out = combine(out, [a[2] if k == 4 else None for k in range(count)], plus)
        return out

    residual = [(one, zero)] + [None] * (count - 1)
    answer = [None] * count
    directions, images, lows, curvatures = [], [], [], []
    for iteration in range(ITERS):
        direction = residual
        image = apply(direction, iteration == 0)
        factors = [over(inner(image, low), c) for low, c in zip(lows, curvatures)]
        factors = [(f[0], -f[1]) for f in factors]
        for f, p, q in zip(factors, directions, images):
            image = combine(image, scale(f, q), minus)
            direction = combine(direction, scale(f, p), minus)
        low = lower(image)
        curvature = inner(image, low)[0]
        along = inner(residual, low)
        step = over((along[0], -along[1]), curvature)
        answer = combine(answer, scale(step, direction), plus)
        residual = combine(residual, scale(step, image), minus)
        directions.append(direction)
        images.append(image)
        lows.append(low)
        curvatures.append(curvature)
    return answer, residual


def finish_kernel(sums, r0, v1, w1, v2, w2, v3, near, fine_hbm, resid_hbm, coef, mixed, fine, resid, sem, resid_sem):
    sites, rows, wide = r0.shape
    half = wide // 2
    quarter = half // 2
    middle = near.shape[-1] // 2
    dense = sums[0]
    for d in range(1, sums.shape[0]):
        dense = dense + sums[d]
    basis = [r0, v1, w1, v2, w2, v3]
    table = slots(BASIS)
    turned = [dense if g == 0 else pltpu.roll(dense, wide - rows * g, 1) for g in range(-(-len(table) // 8))]
    gram = {key: turned[slot // 8][slot % 8 : slot % 8 + 1] for key, slot in table.items()}
    answer, residual = recurrences(gram, jnp.ones((1, wide), F32))
    entries = []
    for which, coords in ((0, answer), (1, residual)):
        for index, value in enumerate(coords):
            if value is not None:
                entries.append((which, index, value))
    coef[...] = jnp.zeros_like(coef)
    for e, (_, _, value) in enumerate(entries):
        coef[2 * e : 2 * e + 1] = value[0]
        coef[2 * e + 1 : 2 * e + 2] = value[1]
    columns = coef[...].T[:rows]
    sign = jnp.where(lanes((8, wide)) < half, -1.0, 1.0)
    spread = [
        (
            which,
            index,
            jnp.broadcast_to(columns[:, 2 * e : 2 * e + 1], (rows, wide)),
            jnp.broadcast_to(columns[:, 2 * e + 1 : 2 * e + 2], (rows, wide)),
        )
        for e, (which, index, _) in enumerate(entries)
    ]
    low = lanes((8, wide)) < quarter

    def combined(s, block):
        span = slice(8 * block, 8 * block + 8)
        plain = [b[s, span, :] for b in basis]
        out = []
        for which in range(2):
            terms = [(re[span] * plain[i], im[span] * plain[i]) for w, i, re, im in spread if w == which]
            re, im = functools.reduce(plus, terms)
            out.append(re + pltpu.roll(im, half, 1) * sign)
        resid[s, span, :] = out[1]
        x = out[0].astype(BF16).astype(F32)
        by1 = pltpu.roll(x, wide - quarter, 1)
        by2 = pltpu.roll(x, half, 1)
        by3 = pltpu.roll(x, quarter, 1)
        even, odd = pl.ds(16 * block, 8, 2), pl.ds(16 * block + 1, 8, 2)
        mixed[s, 0, even, :] = jnp.where(low, x, -by1)
        mixed[s, 0, odd, :] = jnp.where(low, by2, by3)
        mixed[s, 1, even, :] = jnp.where(low, by1, -by2)
        mixed[s, 1, odd, :] = jnp.where(low, by3, x)

    def prolonged(s):
        for h in range(2):
            cols = slice(h * middle, (h + 1) * middle)
            product = lax.dot_general(
                mixed[s, h, :, :half].astype(BF16), near[s, :, cols], NN, preferred_element_type=F32
            )
            fine[s, :, :, cols] = product.astype(BF16).reshape(rows, 2, middle)

    groups = sem.shape[0]
    copies = []
    for g in range(groups + 1):
        if g < groups and g % WAVE == 0:
            for block in range(rows // 8):
                for s in range(g * EACH, (g + WAVE) * EACH):
                    combined(s, block)
        if g == groups - WAVE:
            copies.append(pltpu.make_async_copy(resid, resid_hbm, resid_sem))
            copies[-1].start()
        if g:
            span = pl.ds((g - 1) * EACH, EACH)
            for s in range((g - 1) * EACH, g * EACH):
                prolonged(s)
            copies.append(pltpu.make_async_copy(fine.at[span], fine_hbm.at[span], sem.at[g - 1]))
            copies[-1].start()
    for copy in copies:
        copy.wait()


def finish(sums, *arrays):
    sites, nrhs, wide = arrays[0].shape
    fine = (sites, nrhs, 2, arrays[-1].shape[-1])
    return pl.pallas_call(
        finish_kernel,
        in_specs=[VM] * 8,
        out_specs=[HBM, HBM],
        out_shape=[jax.ShapeDtypeStruct(fine, BF16), jax.ShapeDtypeStruct((sites, nrhs, wide), F32)],
        scratch_shapes=[
            pltpu.VMEM((wide, wide), F32),
            pltpu.VMEM((sites, 2, 2 * nrhs, wide), F32),
            pltpu.VMEM(fine, BF16),
            pltpu.VMEM((sites, nrhs, wide), F32),
            pltpu.SemaphoreType.DMA((sites // EACH,)),
            pltpu.SemaphoreType.DMA,
        ],
        compiler_params=PARAMS,
        name="finish",
    )(sums, *arrays)


def on_device(fine_residual, near_null, coarse_operator):
    ly, lx, nrhs, _, fine = fine_residual.shape[2:]
    sites = ly * lx
    nvec = near_null.shape[-2]
    wide = 4 * nvec
    field = fine_residual.reshape(sites, nrhs, 2, fine)
    near = near_null.reshape(sites, 2 * nvec, fine)
    oper = coarse_operator.reshape((-1, sites) + coarse_operator.shape[-2:])
    dims = (ly, lx)
    field, near, oper = (pltpu.with_memory_space_constraint(a, pltpu.HBM) for a in (field, near, oper))
    vector = jax.ShapeDtypeStruct((sites, nrhs, wide), F32)
    rounded = jax.ShapeDtypeStruct((sites, nrhs, wide), BF16)
    xy = pltpu.VMEM((sites, 2 * nrhs, wide), BF16)

    r0, h0, l0, near = restrict(field, near)

    planes = exchange(h0)
    part, w1, oper = pl.pallas_call(
        functools.partial(first_local_kernel, dims),
        in_specs=[VM, VM, HBM],
        out_specs=[VM] * 3,
        out_shape=[vector, vector, jax.ShapeDtypeStruct(oper.shape[1:], BF16)],
        scratch_shapes=[xy, pltpu.SemaphoreType.DMA],
        compiler_params=PARAMS,
        name="local_1",
    )(h0, l0, oper)
    v1, h1, l1 = pl.pallas_call(
        halo_kernel,
        in_specs=[VM] * 7,
        out_specs=[VM] * 3,
        out_shape=[vector, rounded, rounded],
        compiler_params=PARAMS,
        name="halo_1",
    )(*planes, part, r0, oper)

    planes = exchange(h1)
    part, w2 = pl.pallas_call(
        functools.partial(second_local_kernel, dims),
        in_specs=[VM] * 4,
        out_specs=[VM] * 2,
        out_shape=[vector, vector],
        scratch_shapes=[xy],
        compiler_params=PARAMS,
        name="local_2",
    )(h1, l1, w1, oper)
    v2, h2, l2 = pl.pallas_call(
        halo_kernel,
        in_specs=[VM] * 7,
        out_specs=[VM] * 3,
        out_shape=[vector, rounded, rounded],
        compiler_params=PARAMS,
        name="halo_2",
    )(*planes, part, v1, oper)

    planes = exchange(h2)
    part, early = pl.pallas_call(
        functools.partial(third_local_kernel, dims),
        in_specs=[VM] * 8,
        out_specs=[VM] * 2,
        out_shape=[vector, jax.ShapeDtypeStruct((nrhs, wide), F32)],
        scratch_shapes=[xy],
        compiler_params=PARAMS,
        name="local_3",
    )(h2, l2, r0, v1, w1, v2, w2, oper)
    devices = lax.axis_size("grp") * lax.axis_size("dev")
    v3, sums = pl.pallas_call(
        last_kernel,
        in_specs=[VM] * 12,
        out_specs=[VM] * 2,
        out_shape=[vector, jax.ShapeDtypeStruct((devices, 8, wide), F32)],
        compiler_params=PARAMS,
        name="halo_3",
    )(*planes, part, r0, v1, w1, v2, w2, early, oper)

    sums = lax.all_to_all(sums, ("grp", "dev"), 0, 0)
    correction, residual = finish(sums, r0, v1, w1, v2, w2, v3, near)
    return correction.reshape(fine_residual.shape), residual.reshape((1, 1, ly, lx, nrhs, wide))


def solution(mesh):
    in_specs = (
        P("grp", "dev", None, None, None, None, None),
        P("grp", "dev", None, None, None, None, None),
        P(None, "dev", None, None, None, None),
    )
    out_specs = (
        P("grp", "dev", None, None, None, None, None),
        P("grp", "dev", None, None, None, None),
    )
    return jax.shard_map(
        on_device, mesh=mesh, in_specs=in_specs, out_specs=out_specs, check_vma=False
    )
```

```python
import functools

import jax
import jax.numpy as jnp
from jax import lax
from jax.experimental import pallas as pl
from jax.experimental.pallas import tpu as pltpu
from jax.sharding import PartitionSpec as P

ITERS = 3
BASIS = 6
SHIFT = 3.0
EACH = 2
WAVE = 2
LIMIT = 16 * 1024 * 1024
F32 = jnp.float32
BF16 = jnp.bfloat16
NT = (((1,), (1,)), ((), ()))
NN = (((1,), (0,)), ((), ()))
VM = pl.BlockSpec(memory_space=pltpu.VMEM)
HBM = pl.BlockSpec(memory_space=pltpu.HBM)
PARAMS = pltpu.CompilerParams(vmem_limit_bytes=LIMIT)


def pairings(count, ring=False):
    if ring or count % 2:
        ahead = [(i, (i - 1) % count) for i in range(count)]
        return ahead, [(target, source) for source, target in ahead]
    first = [(i, i ^ 1) for i in range(count)]
    second = [(i, (i + 1) % count if i % 2 else (i - 1) % count) for i in range(count)]
    return first, second


def swapped(axis):
    if lax.axis_size(axis) % 2:
        return jnp.bool_(False)
    return lax.rem(lax.axis_index(axis), 2) == 1


def exchange(high):
    z_first, z_second = pairings(lax.axis_size("dev"))
    t_first, t_second = pairings(lax.axis_size("grp"), True)
    t_two = lax.ppermute(high, "grp", t_second)
    z_two = lax.ppermute(high, "dev", z_second)
    z_one = lax.ppermute(high, "dev", z_first)
    t_one = lax.ppermute(high, "grp", t_first)
    return t_two, t_one, z_one, z_two


def lanes(shape):
    return lax.broadcasted_iota(jnp.int32, shape, len(shape) - 1)


def stacked(vector):
    wide = vector.astype(F32)
    half = wide.shape[-1] // 2
    turned = pltpu.roll(wide, half, 1)
    sign = jnp.where(lanes(wide.shape) < half, 1.0, -1.0)
    return jnp.concatenate([wide * sign, turned], axis=0).astype(BF16)


def halves(value):
    high = value.astype(BF16)
    return high, (value - high.astype(F32)).astype(BF16)


def joined(product, rows):
    return jnp.concatenate([product[:rows], product[rows:]], axis=1)


def batches(sites):
    return [(s, EACH) for s in range(0, sites, EACH)]


def restrict_kernel(
    field_hbm, near_hbm, source_ref, high_ref, low_ref, near_ref, field, prods, sem
):
    sites, nrhs = field.shape[:2]
    middle = field.shape[-1] // 2
    nvec = near_ref.shape[1] // 2
    wide = 4 * nvec
    groups = batches(sites)
    copies = []
    for g, (first, count) in enumerate(groups):
        span = pl.ds(first, count)
        pair = (
            pltpu.make_async_copy(field_hbm.at[span], field.at[span], sem.at[0, g]),
            pltpu.make_async_copy(near_hbm.at[span], near_ref.at[span], sem.at[1, g]),
        )
        for copy in pair:
            copy.start()
        copies.append(pair)
    lane = lanes((nrhs, wide))

    def multiply(s):
        fine = field[s].reshape(2 * nrhs, 2 * middle)
        near = near_ref[s]
        parts = [
            lax.dot_general(
                fine[:, h * middle : (h + 1) * middle],
                near[:, h * middle : (h + 1) * middle],
                NT,
                preferred_element_type=F32,
            )
            for h in range(2)
        ]
        prods[s] = jnp.concatenate(parts, axis=1)

    def arrange(s):
        even = prods[s, pl.ds(0, nrhs, 2), :]
        odd = prods[s, pl.ds(1, nrhs, 2), :]
        real = even + pltpu.roll(odd, wide - nvec, 1)
        imag = odd - pltpu.roll(even, wide - nvec, 1)
        value = jnp.where(
            lane < nvec,
            real,
            jnp.where(
                lane < 2 * nvec,
                pltpu.roll(real, wide - nvec, 1),
                jnp.where(lane < 3 * nvec, pltpu.roll(imag, 2 * nvec, 1), pltpu.roll(imag, nvec, 1)),
            ),
        )
        source_ref[s] = value
        high_ref[s], low_ref[s] = halves(value)

    for g in range(len(groups) + 1):
        if g < len(groups):
            for copy in copies[g]:
                copy.wait()
            for s in range(groups[g][0], sum(groups[g])):
                multiply(s)
        if g:
            for s in range(groups[g - 1][0], sum(groups[g - 1])):
                arrange(s)


def restrict(field, near):
    sites, nrhs, _, fine = field.shape
    coarse = 2 * near.shape[1]
    return pl.pallas_call(
        restrict_kernel,
        in_specs=[HBM] * 2,
        out_specs=[VM] * 4,
        out_shape=[
            jax.ShapeDtypeStruct((sites, nrhs, coarse), F32),
            jax.ShapeDtypeStruct((sites, nrhs, coarse), BF16),
            jax.ShapeDtypeStruct((sites, nrhs, coarse), BF16),
            jax.ShapeDtypeStruct(near.shape, BF16),
        ],
        scratch_shapes=[
            pltpu.VMEM(field.shape, BF16),
            pltpu.VMEM((sites, 2 * nrhs, coarse), F32),
            pltpu.SemaphoreType.DMA((2, len(batches(sites)))),
        ],
        compiler_params=PARAMS,
        name="restrict",
    )(field, near)


def neighbours(s, ly, lx):
    y, x = s // lx, s % lx
    return [((y + 1) % ly) * lx + x, ((y - 1) % ly) * lx + x, y * lx + (x + 1) % lx, y * lx + (x - 1) % lx]


def local_product(s, dims, blocks, xy, extra):
    rows = xy.shape[1]
    wide = xy.shape[2]
    centre = lax.dot_general(
        jnp.concatenate([xy[s]] + [stacked(e) for e in extra], axis=0),
        blocks[:, :wide],
        NT,
        preferred_element_type=F32,
    )
    sides = lax.dot_general(
        jnp.concatenate([xy[j] for j in neighbours(s, *dims)], axis=1),
        blocks[:, 5 * wide :],
        NT,
        preferred_element_type=F32,
    )
    total = centre[:rows] + sides
    return total, [centre[(i + 1) * rows : (i + 2) * rows] for i in range(len(extra))]


def first_local_kernel(dims, high, low, oper_hbm, part_ref, rest_ref, oper_ref, xy, sem):
    copy = pltpu.make_async_copy(oper_hbm.at[lax.axis_index("grp")], oper_ref, sem)
    copy.start()
    sites = xy.shape[0]
    rows = high.shape[1]
    for s in range(sites):
        xy[s] = stacked(high[s])
    copy.wait()
    for s in range(sites):
        total, extra = local_product(s, dims, oper_ref[s], xy, [low[s]])
        part_ref[s] = joined(total, rows)
        rest_ref[s] = joined(extra[0], rows)


def second_local_kernel(dims, high, low, rest, oper_ref, part_ref, rest_ref, xy):
    sites = xy.shape[0]
    rows = high.shape[1]
    for s in range(sites):
        xy[s] = stacked(high[s])
    for s in range(sites):
        total, more = local_product(s, dims, oper_ref[s], xy, [low[s], rest[s]])
        part_ref[s] = joined(total + more[0], rows)
        rest_ref[s] = joined(more[1], rows)


def third_local_kernel(dims, high, low, r0, v1, w1, v2, w2, oper_ref, part_ref, sums_ref, xy):
    sites = xy.shape[0]
    rows = high.shape[1]
    for s in range(sites):
        xy[s] = stacked(high[s])
    for s in range(sites):
        total, more = local_product(s, dims, oper_ref[s], xy, [low[s]])
        part_ref[s] = joined(total + more[0], rows)
    basis = [r0, v1, w1, v2, w2]
    sums_ref[...] = inner_sums(basis, {k: i for k, i in slots(BASIS).items() if k[1] < BASIS - 1})


def halo_value(s, flips, planes, part, before, oper_ref):
    rows, wide = part.shape[1], part.shape[2]
    cols = []
    for flip, (one, two) in zip(flips, planes):
        a, b = one[s].astype(F32), two[s].astype(F32)
        cols.append(stacked(jnp.where(flip, b, a)))
        cols.append(stacked(jnp.where(flip, a, b)))
    product = lax.dot_general(
        jnp.concatenate(cols, axis=1), oper_ref[s, :, wide : 5 * wide], NT, preferred_element_type=F32
    )
    return part[s] + joined(product, rows) - SHIFT * before[s]


def halo_kernel(t_two, t_one, z_one, z_two, part, before, oper_ref, value_ref, high_ref, low_ref):
    flips = (jnp.bool_(False), swapped("dev"))
    for s in range(part.shape[0]):
        value = halo_value(s, flips, ((t_one, t_two), (z_one, z_two)), part, before, oper_ref)
        value_ref[s] = value
        high_ref[s], low_ref[s] = halves(value)


def slots(count):
    table = {}
    for i in range(count):
        for j in range(i, count):
            table[(i, j, 0)] = len(table)
            if j > i:
                table[(i, j, 1)] = len(table)
    return table


def inner_sums(basis, table, newest=None):
    sites, rows, wide = basis[0].shape
    half = wide // 2
    total = {key: jnp.zeros((rows, wide), F32) for key in table}
    for s in range(sites):
        plain = [b[s] for b in basis] + ([newest(s)] if newest else [])
        turned = {j: pltpu.roll(plain[j], half, 1) for j in sorted({k[1] for k in table if k[2]})}
        for i, j, imaginary in table:
            total[(i, j, imaginary)] += plain[i] * (turned[j] if imaginary else plain[j])
    lane = lanes((rows, wide))
    sign = jnp.where(lane < half, 1.0, -1.0)
    packed = jnp.zeros((rows, wide), F32)
    for key, slot in table.items():
        value = total[key] * sign if key[2] else total[key]
        packed = jnp.where(lane == slot, jnp.sum(value, axis=1, keepdims=True), packed)
    return packed


def last_kernel(t_two, t_one, z_one, z_two, part, r0, v1, w1, v2, w2, early, oper_ref, v3, sums_ref):
    flips = (jnp.bool_(False), swapped("dev"))
    sites, rows, wide = part.shape
    table = slots(BASIS)

    def newest(s):
        value = halo_value(s, flips, ((t_one, t_two), (z_one, z_two)), part, v2, oper_ref)
        v3[s] = value
        return value

    late = inner_sums([r0, v1, w1, v2, w2], {k: i for k, i in table.items() if k[1] == BASIS - 1}, newest)
    packed = early[...] + late
    square = packed.T
    groups = -(-len(table) // 8)
    pieces = [square[8 * group : 8 * group + 8] for group in range(groups)]
    dense = jnp.concatenate(pieces + [jnp.zeros((8, wide - rows * groups), F32)], axis=1)
    for d in range(sums_ref.shape[0]):
        sums_ref[d] = dense


def times(a, b):
    return (a[0] * b[0] - a[1] * b[1], a[0] * b[1] + a[1] * b[0])


def plus(a, b):
    return (a[0] + b[0], a[1] + b[1])


def minus(a, b):
    return (a[0] - b[0], a[1] - b[1])


def over(a, b):
    return (a[0] / b, a[1] / b)


def combine(a, b, op):
    out = []
    for x, y in zip(a, b):
        if y is None:
            out.append(x)
        elif x is None:
            out.append(y if op is plus else (-y[0], -y[1]))
        else:
            out.append(op(x, y))
    return out


def scale(c, a):
    return [None if x is None else times(c, x) for x in a]


def recurrences(gram, one):
    zero = jnp.zeros_like(one)

    def entry(i, j):
        if i == j:
            return (gram[(i, i, 0)], zero)
        if i < j:
            return (gram[(i, j, 0)], gram[(i, j, 1)])
        return (gram[(j, i, 0)], -gram[(j, i, 1)])

    count = BASIS

    def lower(a):
        out = []
        for i in range(count):
            total = (zero, zero)
            for j in range(count):
                if a[j] is not None:
                    total = plus(total, times(entry(i, j), a[j]))
            out.append(total)
        return out

    def inner(a, lowered):
        total = (zero, zero)
        for x, y in zip(a, lowered):
            if x is not None:
                total = plus(total, times((x[0], -x[1]), y))
        return total

    def apply(a, rounded):
        out = [None] * count
        shift = lambda x: (SHIFT * x[0], SHIFT * x[1])
        for source, target in ((0, 1), (1, 3), (3, 5)):
            if a[source] is not None:
                out = combine(out, [shift(a[source]) if k == source else None for k in range(count)], plus)
                out = combine(out, [a[source] if k == target else None for k in range(count)], plus)
        if a[0] is not None and not rounded:
            out = combine(out, [a[0] if k == 2 else None for k in range(count)], plus)
        if a[2] is not None:
            out = combine(out, [a[2] if k == 4 else None for k in range(count)], plus)
        return out

    residual = [(one, zero)] + [None] * (count - 1)
    answer = [None] * count
    directions, images, lows, curvatures = [], [], [], []
    for iteration in range(ITERS):
        direction = residual
        image = apply(direction, iteration == 0)
        factors = [over(inner(image, low), c) for low, c in zip(lows, curvatures)]
        factors = [(f[0], -f[1]) for f in factors]
        for f, p, q in zip(factors, directions, images):
            image = combine(image, scale(f, q), minus)
            direction = combine(direction, scale(f, p), minus)
        low = lower(image)
        curvature = inner(image, low)[0]
        along = inner(residual, low)
        step = over((along[0], -along[1]), curvature)
        answer = combine(answer, scale(step, direction), plus)
        residual = combine(residual, scale(step, image), minus)
        directions.append(direction)
        images.append(image)
        lows.append(low)
        curvatures.append(curvature)
    return answer, residual


def finish_kernel(sums, r0, v1, w1, v2, w2, v3, near, fine_hbm, resid_hbm, coef, mixed, fine, resid, sem, resid_sem):
    sites, rows, wide = r0.shape
    half = wide // 2
    quarter = half // 2
    middle = near.shape[-1] // 2
    dense = sums[0]
    for d in range(1, sums.shape[0]):
        dense = dense + sums[d]
    basis = [r0, v1, w1, v2, w2, v3]
    table = slots(BASIS)
    turned = [dense if g == 0 else pltpu.roll(dense, wide - rows * g, 1) for g in range(-(-len(table) // 8))]
    gram = {key: turned[slot // 8][slot % 8 : slot % 8 + 1] for key, slot in table.items()}
    answer, residual = recurrences(gram, jnp.ones((1, wide), F32))
    entries = []
    for which, coords in ((0, answer), (1, residual)):
        for index, value in enumerate(coords):
            if value is not None:
                entries.append((which, index, value))
    coef[...] = jnp.zeros_like(coef)
    for e, (_, _, value) in enumerate(entries):
        coef[2 * e : 2 * e + 1] = value[0]
        coef[2 * e + 1 : 2 * e + 2] = value[1]
    columns = coef[...].T[:rows]
    sign = jnp.where(lanes((8, wide)) < half, -1.0, 1.0)
    spread = [
        (
            which,
            index,
            jnp.broadcast_to(columns[:, 2 * e : 2 * e + 1], (rows, wide)),
            jnp.broadcast_to(columns[:, 2 * e + 1 : 2 * e + 2], (rows, wide)),
        )
        for e, (which, index, _) in enumerate(entries)
    ]
    low = lanes((8, wide)) < quarter

    def combined(s, block):
        span = slice(8 * block, 8 * block + 8)
        plain = [b[s, span, :] for b in basis]
        out = []
        for which in range(2):
            terms = [(re[span] * plain[i], im[span] * plain[i]) for w, i, re, im in spread if w == which]
            re, im = functools.reduce(plus, terms)
            out.append(re + pltpu.roll(im, half, 1) * sign)
        resid[s, span, :] = out[1]
        x = out[0].astype(BF16).astype(F32)
        by1 = pltpu.roll(x, wide - quarter, 1)
        by2 = pltpu.roll(x, half, 1)
        by3 = pltpu.roll(x, quarter, 1)
        even, odd = pl.ds(16 * block, 8, 2), pl.ds(16 * block + 1, 8, 2)
        mixed[s, 0, even, :] = jnp.where(low, x, -by1)
        mixed[s, 0, odd, :] = jnp.where(low, by2, by3)
        mixed[s, 1, even, :] = jnp.where(low, by1, -by2)
        mixed[s, 1, odd, :] = jnp.where(low, by3, x)

    def prolonged(s):
        for h in range(2):
            cols = slice(h * middle, (h + 1) * middle)
            product = lax.dot_general(
                mixed[s, h, :, :half].astype(BF16), near[s, :, cols], NN, preferred_element_type=F32
            )
            fine[s, :, :, cols] = product.astype(BF16).reshape(rows, 2, middle)

    groups = sem.shape[0]
    copies = []
    for g in range(groups + 1):
        if g < groups and g % WAVE == 0:
            for block in range(rows // 8):
                for s in range(g * EACH, (g + WAVE) * EACH):
                    combined(s, block)
        if g == groups - WAVE:
            copies.append(pltpu.make_async_copy(resid, resid_hbm, resid_sem))
            copies[-1].start()
        if g:
            span = pl.ds((g - 1) * EACH, EACH)
            for s in range((g - 1) * EACH, g * EACH):
                prolonged(s)
            copies.append(pltpu.make_async_copy(fine.at[span], fine_hbm.at[span], sem.at[g - 1]))
            copies[-1].start()
    for copy in copies:
        copy.wait()


def finish(sums, *arrays):
    sites, nrhs, wide = arrays[0].shape
    fine = (sites, nrhs, 2, arrays[-1].shape[-1])
    return pl.pallas_call(
        finish_kernel,
        in_specs=[VM] * 8,
        out_specs=[HBM, HBM],
        out_shape=[jax.ShapeDtypeStruct(fine, BF16), jax.ShapeDtypeStruct((sites, nrhs, wide), F32)],
        scratch_shapes=[
            pltpu.VMEM((wide, wide), F32),
            pltpu.VMEM((sites, 2, 2 * nrhs, wide), F32),
            pltpu.VMEM(fine, BF16),
            pltpu.VMEM((sites, nrhs, wide), F32),
            pltpu.SemaphoreType.DMA((sites // EACH,)),
            pltpu.SemaphoreType.DMA,
        ],
        compiler_params=PARAMS,
        name="finish",
    )(sums, *arrays)


def on_device(fine_residual, near_null, coarse_operator):
    ly, lx, nrhs, _, fine = fine_residual.shape[2:]
    sites = ly * lx
    nvec = near_null.shape[-2]
    wide = 4 * nvec
    field = fine_residual.reshape(sites, nrhs, 2, fine)
    near = near_null.reshape(sites, 2 * nvec, fine)
    oper = coarse_operator.reshape((-1, sites) + coarse_operator.shape[-2:])
    dims = (ly, lx)
    field, near, oper = (pltpu.with_memory_space_constraint(a, pltpu.HBM) for a in (field, near, oper))
    vector = jax.ShapeDtypeStruct((sites, nrhs, wide), F32)
    rounded = jax.ShapeDtypeStruct((sites, nrhs, wide), BF16)
    xy = pltpu.VMEM((sites, 2 * nrhs, wide), BF16)

    r0, h0, l0, near = restrict(field, near)

    planes = exchange(h0)
    part, w1, oper = pl.pallas_call(
        functools.partial(first_local_kernel, dims),
        in_specs=[VM, VM, HBM],
        out_specs=[VM] * 3,
        out_shape=[vector, vector, jax.ShapeDtypeStruct(oper.shape[1:], BF16)],
        scratch_shapes=[xy, pltpu.SemaphoreType.DMA],
        compiler_params=PARAMS,
        name="local_1",
    )(h0, l0, oper)
    v1, h1, l1 = pl.pallas_call(
        halo_kernel,
        in_specs=[VM] * 7,
        out_specs=[VM] * 3,
        out_shape=[vector, rounded, rounded],
        compiler_params=PARAMS,
        name="halo_1",
    )(*planes, part, r0, oper)

    planes = exchange(h1)
    part, w2 = pl.pallas_call(
        functools.partial(second_local_kernel, dims),
        in_specs=[VM] * 4,
        out_specs=[VM] * 2,
        out_shape=[vector, vector],
        scratch_shapes=[xy],
        compiler_params=PARAMS,
        name="local_2",
    )(h1, l1, w1, oper)
    v2, h2, l2 = pl.pallas_call(
        halo_kernel,
        in_specs=[VM] * 7,
        out_specs=[VM] * 3,
        out_shape=[vector, rounded, rounded],
        compiler_params=PARAMS,
        name="halo_2",
    )(*planes, part, v1, oper)

    planes = exchange(h2)
    part, early = pl.pallas_call(
        functools.partial(third_local_kernel, dims),
        in_specs=[VM] * 8,
        out_specs=[VM] * 2,
        out_shape=[vector, jax.ShapeDtypeStruct((nrhs, wide), F32)],
        scratch_shapes=[xy],
        compiler_params=PARAMS,
        name="local_3",
    )(h2, l2, r0, v1, w1, v2, w2, oper)
    devices = lax.axis_size("grp") * lax.axis_size("dev")
    v3, sums = pl.pallas_call(
        last_kernel,
        in_specs=[VM] * 12,
        out_specs=[VM] * 2,
        out_shape=[vector, jax.ShapeDtypeStruct((devices, 8, wide), F32)],
        compiler_params=PARAMS,
        name="halo_3",
    )(*planes, part, r0, v1, w1, v2, w2, early, oper)

    sums = lax.all_to_all(sums, ("grp", "dev"), 0, 0)
    correction, residual = finish(sums, r0, v1, w1, v2, w2, v3, near)
    return correction.reshape(fine_residual.shape), residual.reshape((1, 1, ly, lx, nrhs, wide))


def solution(mesh):
    in_specs = (
        P("grp", "dev", None, None, None, None, None),
        P("grp", "dev", None, None, None, None, None),
        P(None, "dev", None, None, None, None),
    )
    out_specs = (
        P("grp", "dev", None, None, None, None, None),
        P("grp", "dev", None, None, None, None),
    )
    return jax.shard_map(
        on_device, mesh=mesh, in_specs=in_specs, out_specs=out_specs, check_vma=False
    )
```
